32 devices in a mesh: pipe: 2 (over core), expert: 16 (over z, y, x).
Axes of the slice: x: 2, y: 2, z: 4, core: 2. Of those that a mesh axis runs over, the one named last changes fastest.
Arguments:
- section_inputs: bfloat16 [2, 2048, 7168], P('pipe', 'expert'), may hold values from -6 to 6
- output_grads: bfloat16 [2, 2048, 7168], P('pipe', 'expert'), may hold values from -6 to 6
- w_gate: bfloat16 [2, 7168, 2048], P('pipe', None, 'expert'), may hold values from -0.0625 to 0.0625
- w_up: bfloat16 [2, 7168, 2048], P('pipe', None, 'expert'), may hold values from -0.0625 to 0.0625
- w_down: bfloat16 [2, 2048, 7168], P('pipe', 'expert'), may hold values from -0.125 to 0.125
- route_ids: int32 [2, 2048, 8], P('pipe', 'expert'), may hold values from 0 to 255, all different within a row; in each aligned block of 128 rows (0 to 127, 128 to 255, ..., all dimensions but the last counted through in order) at most 5 rows name the same one
- route_gates: float32 [2, 2048, 8], P('pipe', 'expert'), may hold values from 0.25 to 1
Outputs:
- handed_grads: bfloat16 [2, 2048, 7168], P('pipe', 'expert')
- down_grads: bfloat16 [2, 2048, 7168], P('pipe', 'expert')
The draws below stay inside these ranges and needn't reach their ends.
Inputs may be any that keep to these rules, and one draw needn't show every extreme that they name: `route_ids`: each row names 8 different experts. Within the 128 rows of one device of one section, no expert is named by more than 5 rows.
All inputs are finite; a program needn't handle non-finite values.
Results may differ from the reference program's by a relative error of at most 0.0057.
Values may be sent and summed in bfloat16 or wider, within the bound.
A program may use at most 192 MiB of HBM per device.

```python
import math
import jax
import jax.numpy as jnp
import numpy as np
from jax import lax

D = 7168
FF = 2048
EXPERTS = 256
TOPK = 8
SHARDS = 16
TOK_DEV = 128
CAP = 5
LIVE = 1
TOKENS = 2048
N_EXPERT = 16


def steps_of(rng, extent, pieces, least, high):
    level, own = 1.0, jax.random.fold_in(rng, 6)
    for position, shards_of in pieces:
        draws = jnp.exp(jax.random.uniform(jax.random.fold_in(own, position), (shards_of,), jnp.float32, least / len(pieces), high / len(pieces)))
        level = level * jnp.repeat(draws, extent[position] // shards_of).reshape([-1 if axis == position else 1 for axis in range(len(extent))])
    return level


def assign_block(rng, own, number, rows, number_of, top, reach, lean):
    ranking = jax.random.permutation(rng, number_of)
    crowded, usual = shares(number_of, rows * top, reach, lean, True), shares(number_of, rows * top, reach, lean, False)
    places = jnp.arange(number_of)

    def named(lengths, offset_by):
        used = int((lengths > 0).sum())
        fixed = max(1, used // 4)
        shifted = fixed + (places - fixed + offset_by * (used - fixed)) % max(1, number_of - fixed)
        return jnp.zeros((number_of,), jnp.int32).at[ranking[jnp.where(places < fixed, places, shifted)]].set(jnp.asarray(lengths, jnp.int32))

    lengths = jnp.where(number % 4 == 0, named(crowded, number // 4), named(usual, number - number // 4 - 1))
    mixed = jax.random.permutation(jax.random.fold_in(own, 3), number_of)
    donor, taker = mixed[0:number_of // 2 * 2:2], mixed[1:number_of // 2 * 2:2]
    margin = jnp.minimum(lengths[donor] - 1, reach - lengths[taker]) // 2
    margin = jnp.where((donor == ranking[0]) | (taker == ranking[0]) | (lengths[taker] == 0), 0, jnp.maximum(margin, 0))
    shifted = jax.random.randint(jax.random.fold_in(own, 4), (number_of // 2,), 0, 1 << 20) % (margin + 1)
    lengths = lengths.at[donor].add(-shifted).at[taker].add(shifted)
    labels = jnp.searchsorted(jnp.cumsum(lengths), jnp.arange(rows * top), side="right").astype(jnp.int32)
    grid = labels.reshape(top, rows).T
    grid = grid[jax.random.permutation(jax.random.fold_in(own, 1), rows)]
    offset_by = jax.random.randint(jax.random.fold_in(own, 2), (rows, 1), 0, top)
    return jnp.take_along_axis(grid, (jnp.arange(top)[None, :] + offset_by) % top, axis=1)


def shares(amount, total, most, lean, full):
    weights = [(1 << 20) // math.isqrt(grade ** lean) + 1 for grade in range(1, amount + 1)]
    largest = most if full else min(most, max(-(-total // amount), total * weights[0] // sum(weights)))
    least = 1 if total - largest >= amount - 1 else 0
    counts, surplus = [largest] + [least] * (amount - 1), total - largest - least * (amount - 1)
    while surplus > 0:
        free = [i for i in range(1, amount) if counts[i] < largest] or [i for i in range(1, amount) if counts[i] < most]
        whole, budget = sum([weights[i] for i in free]), surplus
        for i in free:
            more = min(most - counts[i], max(1, budget * weights[i] // whole), surplus)
            counts[i] = counts[i] + more
            surplus = surplus - more
    return np.array(counts)


def scatter_about(own_key, extent, deviation, bound, shards=(), kind=jnp.bfloat16):
    result = jax.random.normal(own_key, extent, jnp.float32) * deviation
    if len(shards) > 0:
        result = steps_of(own_key, extent, shards, -0.22, 0.18) * result
    return jnp.clip(result, min=-bound, max=bound).astype(kind)


def setup_inputs(seed: int = 0) -> dict:
    splits = jax.random.split(jax.random.key(seed), 8)
    section_inputs = scatter_about(splits[0], (2, TOKENS, D), 1.0, 6.0, ((0, 2), (1, 16)))
    output_grads = scatter_about(splits[1], (2, TOKENS, D), 1.0, 6.0, ((0, 2), (1, 16)))
    w_gate = scatter_about(splits[2], (2, D, LIVE * FF), D ** -0.5, 0.0625, ((0, 2), (2, 16)))
    w_up = scatter_about(splits[3], (2, D, LIVE * FF), D ** -0.5, 0.0625, ((0, 2), (2, 16)))
    w_down = scatter_about(splits[4], (2, LIVE * FF, D), FF ** -0.5, 0.125, ((0, 2), (1, 16)))
    route_ids_keys = jax.random.split(jax.random.fold_in(splits[5], 1), 2 * TOKENS // TOK_DEV)
    route_ids_turns = jax.random.permutation(jax.random.fold_in(splits[5], 3), 2 * TOKENS // TOK_DEV)
    route_ids = jax.vmap(lambda own, number: assign_block(jax.random.fold_in(splits[5], 2), own, number, TOK_DEV, EXPERTS, TOPK, CAP, 2))(route_ids_keys, route_ids_turns).reshape((2, TOKENS, TOPK))
    route_gates = jnp.clip(0.25 + 0.75 * jax.random.uniform(splits[6], (2, TOKENS, TOPK), jnp.float32) ** steps_of(splits[6], (2, TOKENS, TOPK), ((0, 2), (1, 16)), -0.2, 0.2), 0.25, 1.0)
    return dict(section_inputs=section_inputs, output_grads=output_grads, w_gate=w_gate, w_up=w_up, w_down=w_down, route_ids=route_ids, route_gates=route_gates)


def one_section(inputs, grads, route, gate, w_gate, w_up, w_down):
    limit = N_EXPERT * CAP
    block_width = FF // SHARDS
    zero_row = jnp.zeros((1, D), jnp.bfloat16)
    inputs_pad = jnp.concatenate([inputs, zero_row], 0)
    grads_pad = jnp.concatenate([grads, zero_row], 0)

    def step(branch, expert):
        hit = route == expert
        chosen = jnp.any(hit, axis=1)
        weight = jnp.sum(jnp.where(hit, gate, jnp.float32(0.0)), axis=1)
        weight_pad = jnp.concatenate([weight, jnp.zeros((1,), jnp.float32)])
        index = jnp.nonzero(chosen, size=limit, fill_value=TOKENS)[0].astype(jnp.int32)
        rows_in = inputs_pad[index]
        rows_grad = (weight_pad[index][:, None] * grads_pad[index].astype(jnp.float32)).astype(jnp.bfloat16)
        start = (expert * FF).astype(jnp.int32)
        gate_cols = lax.dynamic_slice_in_dim(w_gate, start, FF, 1)
        up_cols = lax.dynamic_slice_in_dim(w_up, start, FF, 1)
        down_rows = lax.dynamic_slice_in_dim(w_down, start, FF, 0)
        gate_pre = jnp.dot(rows_in, gate_cols, preferred_element_type=jnp.float32)
        up_pre = jnp.dot(rows_in, up_cols, preferred_element_type=jnp.float32)
        sigma = jax.nn.sigmoid(gate_pre)
        silu_gate = gate_pre * sigma
        hidden = (silu_gate * up_pre).astype(jnp.bfloat16)
        back_hidden = jnp.dot(rows_grad, down_rows.T, preferred_element_type=jnp.float32)
        grad_gate = (back_hidden * up_pre * sigma * (1.0 + gate_pre * (1.0 - sigma))).astype(jnp.bfloat16)
        grad_up = (back_hidden * silu_gate).astype(jnp.bfloat16)
        part_gate = jnp.einsum("lsh,dsh->lsd", grad_gate.astype(jnp.float32).reshape(limit, SHARDS, block_width), gate_cols.astype(jnp.float32).reshape(D, SHARDS, block_width))
        part_up = jnp.einsum("lsh,dsh->lsd", grad_up.astype(jnp.float32).reshape(limit, SHARDS, block_width), up_cols.astype(jnp.float32).reshape(D, SHARDS, block_width))
        rounded = lax.optimization_barrier((part_gate + part_up).astype(jnp.bfloat16))
        summed = jnp.sum(rounded.astype(jnp.float32), axis=1)
        branch = branch.at[index].add(summed)
        down_part = jnp.dot(hidden.T, rows_grad, preferred_element_type=jnp.float32).astype(jnp.bfloat16)
        return branch, down_part

    branch, downs = lax.scan(step, jnp.zeros((TOKENS + 1, D), jnp.float32), jnp.arange(LIVE, dtype=jnp.int32))
    input_grad = (grads.astype(jnp.float32) + branch[:TOKENS]).astype(jnp.bfloat16)
    return input_grad, downs.reshape(LIVE * FF, D)


def reference(section_inputs, output_grads, w_gate, w_up, w_down, route_ids, route_gates):
    first_grad, first_down = one_section(section_inputs[0], output_grads[0], route_ids[0], route_gates[0], w_gate[0], w_up[0], w_down[0])
    second_grad, second_down = one_section(section_inputs[1], output_grads[1], route_ids[1], route_gates[1], w_gate[1], w_up[1], w_down[1])
    handed_grads = jnp.stack([second_grad, first_grad])
    down_grads = jnp.stack([first_down, second_down])
    return (handed_grads, down_grads)
```

```python
import jax
import jax.numpy as jnp
from jax import lax
from jax.experimental import pallas as pl
from jax.experimental.pallas import tpu as pltpu
from jax.sharding import PartitionSpec as P

SHARDS = 16
CAP = 5
PIECES = 8
MESH = pl.DeviceIdType.MESH
CONTRACT_LAST = (((1,), (1,)), ((), ()))
ROWS_FIRST = (((0,), (0,)), ((), ()))


def hidden_grads(gate_pre, up_pre, back_hidden):
    sigma = jax.nn.sigmoid(gate_pre)
    silu_gate = gate_pre * sigma
    hidden = silu_gate * up_pre
    grad_gate = back_hidden * up_pre * sigma * (1.0 + gate_pre * (1.0 - sigma))
    grad_up = back_hidden * silu_gate
    return hidden, grad_gate, grad_up


def flip(z, k):
    if k == 0:
        return z
    if k == 1:
        return z + 1 - 2 * lax.rem(z, 2)
    if k == 2:
        return lax.rem(z + 2, 4)
    return 3 - z


def group_kernel(
    x_hbm, g_hbm, wg_hbm, wu_hbm, wd_hbm, route_ref, gate_ref, perm_ref, unperm_ref,
    rows_out, down_out,
    x_v, g_v, wgu, wd_v, staged, plain, plain_in, gath, xf, gf, pfull, part, diag_in,
    fwd_x, fwd_y, in_x, in_y, zsum, in_z, down_v, rows_v,
    load_sem, out_sem, z_send, z_recv, xy_send, xy_recv, d_send, d_recv, p_send, p_recv,
    s1_send, s1_recv, s2_send, s2_recv, s3_send, s3_recv,
):
    slots, piece = staged.shape[0], staged.shape[2]
    block = wd_v.shape[0]
    pipe = lax.axis_index("pipe")
    me = lax.axis_index("expert")
    base = (me // SHARDS) * SHARDS
    local = lax.rem(me, SHARDS)
    z = local // 4
    xy = lax.rem(local, 4)
    y, x = xy // 2, lax.rem(xy, 2)
    at_x, at_y, at_d = y * 2 + 1 - x, (1 - y) * 2 + x, 3 - xy

    def device(p, zz, spot):
        return {"pipe": p, "expert": base + zz * 4 + spot}

    x_dev, y_dev = device(pipe, z, at_x), device(pipe, z, at_y)
    z_dev = [device(pipe, flip(z, k), xy) for k in range(4)]
    back_dev = [device(1 - pipe, flip(z, k), xy) for k in range(4)]

    barrier = pltpu.get_barrier_semaphore()
    for other in [x_dev, y_dev] + z_dev[1:] + back_dev:
        pl.semaphore_signal(barrier, inc=1, device_id=other, device_id_type=MESH)

    loads = [
        pltpu.make_async_copy(x_hbm, x_v, load_sem.at[0]),
        pltpu.make_async_copy(g_hbm, g_v, load_sem.at[1]),
        pltpu.make_async_copy(wg_hbm, wgu.at[:, :, pl.ds(0, block)], load_sem.at[2]),
        pltpu.make_async_copy(wu_hbm, wgu.at[:, :, pl.ds(block, block)], load_sem.at[3]),
        pltpu.make_async_copy(wd_hbm, wd_v, load_sem.at[4]),
    ]
    for copy in loads:
        copy.start()

    tok = route_ref.shape[1]
    hit = route_ref[...] == 0
    member = jnp.sum(jnp.where(hit, 1.0, 0.0), axis=0, keepdims=True)
    weight = jnp.sum(jnp.where(hit, gate_ref[...], 0.0), axis=0, keepdims=True)
    earlier = lax.broadcasted_iota(jnp.int32, (tok, tok), 0) < lax.broadcasted_iota(
        jnp.int32, (tok, tok), 1
    )
    member8 = jnp.broadcast_to(member, (8, tok))
    position = jnp.dot(
        member8.astype(jnp.bfloat16),
        jnp.where(earlier, 1.0, 0.0).astype(jnp.bfloat16),
        preferred_element_type=jnp.float32,
    )
    slot = lax.broadcasted_iota(jnp.int32, (8, tok), 0).astype(jnp.float32)
    pick = jnp.where((member8 == 1.0) & (position == slot), 1.0, 0.0)
    coef = jnp.sum(pick * weight, axis=1, keepdims=True)
    pick_mat = pick.astype(jnp.bfloat16)

    for kind in range(2):
        loads[kind].wait()
        source = x_v if kind == 0 else g_v
        for q in range(PIECES):
            rows = jnp.dot(
                pick_mat, source[:, q * piece:(q + 1) * piece], preferred_element_type=jnp.float32
            )
            scaled = rows if kind == 0 else rows * coef
            for i in range(slots):
                staged[i, kind * PIECES + q:kind * PIECES + q + 1, :] = scaled[i:i + 1, :]
                if kind == 1:
                    plain[i, q:q + 1, :] = rows[i:i + 1, :]
    own = xy * 4 + z
    for i in range(slots):
        gath[own, i] = staged[i].astype(jnp.bfloat16)
    plain_in[0] = plain[...].astype(jnp.bfloat16)

    pl.semaphore_wait(barrier, 9)

    def remote(src, dst, send, recv, to):
        return pltpu.make_async_remote_copy(
            src_ref=src, dst_ref=dst, send_sem=send, recv_sem=recv, device_id=to,
            device_id_type=MESH,
        )

    def halves(k):
        cut = 3 if k % 2 == 0 else 2
        return (pl.ds(0, cut), pl.ds(cut, slots - cut))

    sent = []

    def start(copy):
        copy.start()
        sent.append(copy)
        return copy

    arrivals_z = {}
    for k in (1, 3, 2):
        arrivals_z[k] = start(
            remote(gath.at[own], gath.at[own], z_send.at[k], z_recv.at[k], z_dev[k])
        )

    def slab(spot, k, half):
        return gath.at[spot * 4 + flip(z, k), halves(k)[half]]

    def to_plane(k):
        for half in range(2):
            start(remote(slab(xy, k, half), slab(xy, k, half), xy_send.at[0, k, half],
                         xy_recv.at[0, k, half], x_dev))
            start(remote(slab(xy, k, 1 - half), slab(xy, k, 1 - half),
                         xy_send.at[1, k, 1 - half], xy_recv.at[1, k, 1 - half], y_dev))

    def arrived(axis, k, half):
        spot = at_x if axis == 0 else at_y
        remote(slab(spot, k, half), slab(spot, k, half), xy_send.at[axis, k, half],
               xy_recv.at[axis, k, half], x_dev).wait_recv()

    def to_corner(k):
        arrived(0, k, 0)
        start(remote(slab(at_x, k, 0), slab(at_x, k, 0), d_send.at[k, 0], d_recv.at[k, 0], y_dev))
        arrived(1, k, 1)
        start(remote(slab(at_y, k, 1), slab(at_y, k, 1), d_send.at[k, 1], d_recv.at[k, 1], x_dev))

    to_plane(0)
    plain_copy = start(
        remote(plain_in.at[0], plain_in.at[1], p_send, p_recv, back_dev[0])
    )
    before = 0
    for k in (1, 3, 2):
        spot = gath.at[xy * 4 + flip(z, k)]
        remote(spot, spot, z_send.at[k], z_recv.at[k], z_dev[k]).wait_recv()
        to_plane(k)
        to_corner(before)
        before = k
    to_corner(before)
    for copy in loads[2:]:
        copy.wait()
    for k in (0, 1, 3, 2):
        arrived(0, k, 1)
        arrived(1, k, 0)
        for half in range(2):
            remote(slab(at_d, k, half), slab(at_d, k, half), d_send.at[k, half],
                   d_recv.at[k, half], y_dev).wait_recv()

    for i in range(slots):
        packed = gath[:, i].reshape(SHARDS * 2 * PIECES, piece)
        ordered = jnp.dot(
            perm_ref[...], packed, preferred_element_type=jnp.float32
        ).astype(jnp.bfloat16)
        for q in range(PIECES):
            xf[q, i * SHARDS:(i + 1) * SHARDS, :] = ordered[q * SHARDS:(q + 1) * SHARDS]
            gf[q, i * SHARDS:(i + 1) * SHARDS, :] = ordered[
                (PIECES + q) * SHARDS:(PIECES + q + 1) * SHARDS
            ]

    rows_all = slots * SHARDS
    pre = jnp.zeros((rows_all, 2 * block), jnp.float32)
    back = jnp.zeros((rows_all, block), jnp.float32)
    for q in range(PIECES):
        pre = pre + jnp.dot(xf[q], wgu[q], preferred_element_type=jnp.float32)
        back = back + lax.dot_general(
            gf[q], wd_v[:, q * piece:(q + 1) * piece], CONTRACT_LAST,
            preferred_element_type=jnp.float32,
        )
    hidden, grad_gate, grad_up = hidden_grads(pre[:, :block], pre[:, block:], back)
    grad_both = jnp.concatenate(
        [grad_gate.astype(jnp.bfloat16), grad_up.astype(jnp.bfloat16)], axis=1
    )
    for q in range(PIECES):
        share = lax.dot_general(
            grad_both, wgu[q], CONTRACT_LAST, preferred_element_type=jnp.float32
        ).astype(jnp.bfloat16)
        for i in range(slots):
            pfull[i, q * SHARDS:(q + 1) * SHARDS, :] = share[i * SHARDS:(i + 1) * SHARDS]

    low, high = pl.ds(0, 2), pl.ds(2, 2)
    for i in range(slots):
        units = jnp.dot(
            unperm_ref[...], pfull[i], preferred_element_type=jnp.float32
        ).astype(jnp.bfloat16)
        part[i] = units.reshape(4, 4, PIECES, piece)
        start(remote(part.at[i, at_d, low], diag_in.at[i, low], s1_send.at[i, 0],
                     s1_recv.at[i, 0], y_dev))
        start(remote(part.at[i, at_d, high], diag_in.at[i, high], s1_send.at[i, 1],
                     s1_recv.at[i, 1], x_dev))
    for i in range(slots):
        start(remote(part.at[i, at_x, high], in_x.at[i, high], s1_send.at[i, 2],
                     s1_recv.at[i, 2], x_dev))
        start(remote(part.at[i, at_y, low], in_y.at[i, low], s1_send.at[i, 3],
                     s1_recv.at[i, 3], y_dev))

    hidden_t = jnp.transpose(hidden).astype(jnp.bfloat16)

    def down_piece(q):
        down_v[:, q * piece:(q + 1) * piece] = jnp.dot(
            hidden_t, gf[q], preferred_element_type=jnp.float32
        ).astype(jnp.bfloat16)

    for q in range(PIECES // 2):
        down_piece(q)

    for i in range(slots):
        remote(part.at[i, at_d, low], diag_in.at[i, low], s1_send.at[i, 0],
               s1_recv.at[i, 0], y_dev).wait_recv()
        fwd_x[i] = (
            part[i, at_x, low].astype(jnp.float32) + diag_in[i, low].astype(jnp.float32)
        ).astype(jnp.bfloat16)
        start(remote(fwd_x.at[i], in_x.at[i, low], s2_send.at[i, 0], s2_recv.at[i, 0], x_dev))
        remote(part.at[i, at_d, high], diag_in.at[i, high], s1_send.at[i, 1],
               s1_recv.at[i, 1], x_dev).wait_recv()
        fwd_y[i] = (
            part[i, at_y, high].astype(jnp.float32) + diag_in[i, high].astype(jnp.float32)
        ).astype(jnp.bfloat16)
        start(remote(fwd_y.at[i], in_y.at[i, high], s2_send.at[i, 1], s2_recv.at[i, 1], y_dev))

    for q in range(PIECES // 2, PIECES):
        down_piece(q)
    down_copy = pltpu.make_async_copy(down_v, down_out, out_sem.at[0])
    down_copy.start()

    for i in range(slots):
        remote(part.at[i, at_x, high], in_x.at[i, high], s1_send.at[i, 2],
               s1_recv.at[i, 2], x_dev).wait_recv()
        remote(part.at[i, at_y, low], in_y.at[i, low], s1_send.at[i, 3],
               s1_recv.at[i, 3], y_dev).wait_recv()
        remote(fwd_x.at[i], in_x.at[i, low], s2_send.at[i, 0], s2_recv.at[i, 0],
               x_dev).wait_recv()
        remote(fwd_y.at[i], in_y.at[i, high], s2_send.at[i, 1], s2_recv.at[i, 1],
               y_dev).wait_recv()
        zsum[i] = (
            part[i, xy].astype(jnp.float32) + in_x[i].astype(jnp.float32)
            + in_y[i].astype(jnp.float32)
        ).astype(jnp.bfloat16)
        for k in (2, 3, 1, 0):
            start(remote(zsum.at[i, flip(z, k)], in_z.at[i, z], s3_send.at[i, k],
                         s3_recv.at[i, k], back_dev[k]))

    plain_copy.wait_recv()
    for i in range(slots):
        total = plain_in[1, i].astype(jnp.float32)
        for k in range(4):
            remote(zsum.at[i, 0], in_z.at[i, flip(z, k)], s3_send.at[i, k],
                   s3_recv.at[i, k], back_dev[k]).wait_recv()
        for zz in range(4):
            total = total + in_z[i, zz].astype(jnp.float32)
        rows_v[i] = total
    rows_copy = pltpu.make_async_copy(rows_v, rows_out, out_sem.at[1])
    rows_copy.start()
    for copy in sent:
        copy.wait_send()
    down_copy.wait()
    rows_copy.wait()


def group_work(inputs, grads, gate_cols, up_cols, down_rows, route, gate):
    tok, width = inputs.shape
    block = gate_cols.shape[1]
    piece = width // PIECES
    bf16 = jnp.bfloat16
    wide = SHARDS * 2 * PIECES
    r, c = lax.broadcasted_iota(jnp.int32, (wide, wide), 0), lax.broadcasted_iota(
        jnp.int32, (wide, wide), 1
    )
    perm = ((r % SHARDS == c // (2 * PIECES)) & (r // SHARDS == c % (2 * PIECES))).astype(bf16)
    half = SHARDS * PIECES
    r, c = r[:half, :half], c[:half, :half]
    unperm = ((r // PIECES == c % SHARDS) & (r % PIECES == c // SHARDS)).astype(bf16)
    whole = pl.BlockSpec(memory_space=pl.ANY)
    vmem = pl.BlockSpec(memory_space=pltpu.VMEM)
    dma = pltpu.SemaphoreType.DMA
    units = pltpu.VMEM((CAP, 4, PIECES, piece), bf16)
    rows, down = pl.pallas_call(
        group_kernel,
        out_shape=(
            jax.ShapeDtypeStruct((CAP, PIECES, piece), jnp.float32),
            jax.ShapeDtypeStruct((block, width), bf16),
        ),
        in_specs=[whole] * 5 + [vmem] * 4,
        out_specs=(whole, whole),
        scratch_shapes=[
            pltpu.VMEM((tok, width), bf16),
            pltpu.VMEM((tok, width), bf16),
            pltpu.VMEM((PIECES, piece, 2 * block), bf16),
            pltpu.VMEM((block, width), bf16),
            pltpu.VMEM((CAP, 2 * PIECES, piece), jnp.float32),
            pltpu.VMEM((CAP, PIECES, piece), jnp.float32),
            pltpu.VMEM((2, CAP, PIECES, piece), bf16),
            pltpu.VMEM((SHARDS, CAP, 2 * PIECES, piece), bf16),
            pltpu.VMEM((PIECES, CAP * SHARDS, piece), bf16),
            pltpu.VMEM((PIECES, CAP * SHARDS, piece), bf16),
            pltpu.VMEM((CAP, half, piece), bf16),
            pltpu.VMEM((CAP, 4, 4, PIECES, piece), bf16),
            units,
            pltpu.VMEM((CAP, 2, PIECES, piece), bf16),
            pltpu.VMEM((CAP, 2, PIECES, piece), bf16),
            units,
            units,
            units,
            units,
            pltpu.VMEM((block, width), bf16),
            pltpu.VMEM((CAP, PIECES, piece), jnp.float32),
            dma((5,)), dma((2,)), dma((4,)), dma((4,)), dma((2, 4, 2)), dma((2, 4, 2)),
            dma((4, 2)), dma((4, 2)), dma, dma,
            dma((CAP, 4)), dma((CAP, 4)), dma((CAP, 2)), dma((CAP, 2)),
            dma((CAP, 4)), dma((CAP, 4)),
        ],
        compiler_params=pltpu.CompilerParams(
            collective_id=0, has_side_effects=True, vmem_limit_bytes=48 * 2**20
        ),
        cost_estimate=pl.CostEstimate(
            flops=12 * CAP * SHARDS * width * block, bytes_accessed=14 * tok * width,
            transcendentals=CAP * SHARDS * block,
        ),
        name="relay_group",
    )(
        inputs, grads, gate_cols.reshape(PIECES, piece, block),
        up_cols.reshape(PIECES, piece, block), down_rows, route.T, gate.T, perm, unperm,
    )
    return rows.reshape(CAP, width), down


def plain_work(rows, gate_cols, up_cols, down_rows):
    width = lax.axis_size("expert")
    live = width // SHARDS
    across = [[g * SHARDS + j for g in range(live)] for j in range(SHARDS)]
    within = [[g * SHARDS + j for j in range(SHARDS)] for g in range(live)]
    kinds, count, model_width = rows.shape
    if live > 1:
        rows = lax.all_to_all(
            rows, "expert", split_axis=1, concat_axis=1, tiled=True, axis_index_groups=across
        )
    got = lax.all_gather(rows, "expert", axis=1, tiled=True, axis_index_groups=within)
    flat_in, flat_grad = got[0], got[1]
    gate_pre = jnp.dot(flat_in, gate_cols, preferred_element_type=jnp.float32)
    up_pre = jnp.dot(flat_in, up_cols, preferred_element_type=jnp.float32)
    back = lax.dot_general(flat_grad, down_rows, CONTRACT_LAST, preferred_element_type=jnp.float32)
    hidden, grad_gate, grad_up = hidden_grads(gate_pre, up_pre, back)
    share = lax.dot_general(
        grad_gate.astype(jnp.bfloat16), gate_cols, CONTRACT_LAST,
        preferred_element_type=jnp.float32,
    ) + lax.dot_general(
        grad_up.astype(jnp.bfloat16), up_cols, CONTRACT_LAST, preferred_element_type=jnp.float32
    )
    summed = lax.psum_scatter(
        share.astype(jnp.bfloat16), "expert", scatter_dimension=0, tiled=True,
        axis_index_groups=within,
    )
    if live > 1:
        summed = lax.all_to_all(
            summed, "expert", split_axis=0, concat_axis=0, tiled=True, axis_index_groups=across
        )
    down_part = lax.dot_general(
        hidden.astype(jnp.bfloat16), flat_grad, ROWS_FIRST, preferred_element_type=jnp.float32
    ).astype(jnp.bfloat16)
    return summed, down_part


def slot_picks(route, gate, live):
    hit = route[:, :, None] == jnp.arange(live, dtype=jnp.int32)
    member = jnp.sum(hit.astype(jnp.int32), axis=1)
    weight = jnp.sum(jnp.where(hit, gate[:, :, None], 0.0), axis=1)
    position = jnp.cumsum(member, axis=0) - member
    pick = (member[:, :, None] == 1) & (
        position[:, :, None] == jnp.arange(CAP, dtype=jnp.int32)
    )
    return member, weight, pick


def other_core(value):
    return lax.ppermute(value, "pipe", [(0, 1), (1, 0)])


def body(section_inputs, output_grads, w_gate, w_up, w_down, route_ids, route_gates):
    inputs, grads, route, gate = section_inputs[0], output_grads[0], route_ids[0], route_gates[0]
    gate_cols, up_cols, down_rows = w_gate[0], w_up[0], w_down[0]
    tok_rows = inputs.shape[0]
    live = lax.axis_size("expert") // SHARDS
    if live == 1:
        grads_behind = other_core(grads)
        route_behind = other_core(route)
        rows, down_part = group_work(inputs, grads, gate_cols, up_cols, down_rows, route, gate)
        member, _, pick = slot_picks(route_behind, gate, 1)
        placed = jnp.dot(
            pick.reshape(tok_rows, CAP).astype(jnp.bfloat16), rows.astype(jnp.bfloat16),
            preferred_element_type=jnp.float32,
        )
        handed = jnp.where(member == 1, placed.astype(jnp.bfloat16), grads_behind)
        return handed[None], down_part[None]
    _, weight, pick = slot_picks(route, gate, live)
    pick_mat = pick.astype(jnp.bfloat16).reshape(tok_rows, live * CAP)
    rows_in = lax.dot_general(pick_mat, inputs, ROWS_FIRST, preferred_element_type=jnp.float32)
    chosen = lax.dot_general(pick_mat, grads, ROWS_FIRST, preferred_element_type=jnp.float32)
    slot_gate = jnp.sum(pick.astype(jnp.float32) * weight[:, :, None], axis=0).reshape(-1, 1)
    rows = jnp.stack([rows_in.astype(jnp.bfloat16), (chosen * slot_gate).astype(jnp.bfloat16)])
    summed, down_part = plain_work(rows, gate_cols, up_cols, down_rows)
    branch = jnp.dot(pick_mat, summed, preferred_element_type=jnp.float32)
    input_grad = (grads.astype(jnp.float32) + branch).astype(jnp.bfloat16)
    return other_core(input_grad)[None], down_part[None]


def solution(mesh):
    return jax.shard_map(
        body,
        mesh=mesh,
        in_specs=(
            P("pipe", "expert", None),
            P("pipe", "expert", None),
            P("pipe", None, "expert"),
            P("pipe", None, "expert"),
            P("pipe", "expert", None),
            P("pipe", "expert", None),
            P("pipe", "expert", None),
        ),
        out_specs=(P("pipe", "expert", None), P("pipe", "expert", None)),
        check_vma=False,
    )
```

```python
import jax
import jax.numpy as jnp
from jax import lax
from jax.experimental import pallas as pl
from jax.experimental.pallas import tpu as pltpu
from jax.sharding import PartitionSpec as P

SHARDS = 16
CAP = 5
PIECES = 8
MESH = pl.DeviceIdType.MESH
CONTRACT_LAST = (((1,), (1,)), ((), ()))
ROWS_FIRST = (((0,), (0,)), ((), ()))


def hidden_grads(gate_pre, up_pre, back_hidden):
    sigma = jax.nn.sigmoid(gate_pre)
    silu_gate = gate_pre * sigma
    hidden = silu_gate * up_pre
    grad_gate = back_hidden * up_pre * sigma * (1.0 + gate_pre * (1.0 - sigma))
    grad_up = back_hidden * silu_gate
    return hidden, grad_gate, grad_up


def flip(z, k):
    if k == 0:
        return z
    if k == 1:
        return z + 1 - 2 * lax.rem(z, 2)
    if k == 2:
        return lax.rem(z + 2, 4)
    return 3 - z


def pick_slots(route, gate):
    tok = route.shape[1]
    hit = route == 0
    member = jnp.sum(jnp.where(hit, 1.0, 0.0), axis=0, keepdims=True)
    earlier = lax.broadcasted_iota(jnp.int32, (tok, tok), 0) < lax.broadcasted_iota(
        jnp.int32, (tok, tok), 1
    )
    member8 = jnp.broadcast_to(member, (8, tok))
    position = jnp.dot(
        member8.astype(jnp.bfloat16),
        jnp.where(earlier, 1.0, 0.0).astype(jnp.bfloat16),
        preferred_element_type=jnp.float32,
    )
    slot = lax.broadcasted_iota(jnp.int32, (8, tok), 0).astype(jnp.float32)
    pick = jnp.where((member8 == 1.0) & (position == slot), 1.0, 0.0)
    if gate is None:
        return pick, None
    weight = jnp.sum(jnp.where(hit, gate, 0.0), axis=0, keepdims=True)
    return pick, jnp.sum(pick * weight, axis=1, keepdims=True)


def swap_order(outer, inner):
    size = outer * inner
    r = lax.broadcasted_iota(jnp.int32, (size, size), 0)
    c = lax.broadcasted_iota(jnp.int32, (size, size), 1)
    source = lax.rem(r, outer) * inner + r // outer
    return jnp.where(c == source, 1.0, 0.0).astype(jnp.bfloat16)


def group_kernel(
    x_hbm, g_hbm, wg_hbm, wu_hbm, wd_hbm, route_hbm, gate_hbm,
    rows_out, down_out,
    route_v, gate_v, x_v, g_v, wgu, wd_v, staged, plain, plain_in, gath, xf, gf, pfull, part,
    diag_in, fwd_x, fwd_y, in_x, in_y, zsum, in_z, down_v, rows_v,
    load_sem, out_sem, z_send, z_recv, xy_send, xy_recv, d_send, d_recv, dz_send, dz_recv,
    p_send, p_recv, s1_send, s1_recv, s2_send, s2_recv, s3_send, s3_recv,
):
    slots, piece = staged.shape[0], staged.shape[2]
    block = wd_v.shape[0]
    pipe = lax.axis_index("pipe")
    me = lax.axis_index("expert")
    base = (me // SHARDS) * SHARDS
    local = lax.rem(me, SHARDS)
    z = local // 4
    xy = lax.rem(local, 4)
    y, x = xy // 2, lax.rem(xy, 2)
    at_x, at_y, at_d = y * 2 + 1 - x, (1 - y) * 2 + x, 3 - xy

    def device(p, zz, spot):
        return {"pipe": p, "expert": base + zz * 4 + spot}

    x_dev, y_dev = device(pipe, z, at_x), device(pipe, z, at_y)
    z_dev = [device(pipe, flip(z, k), xy) for k in range(4)]
    back_dev = [device(1 - pipe, flip(z, k), xy) for k in range(4)]

    barrier = pltpu.get_barrier_semaphore()
    for other in [x_dev, y_dev] + z_dev[1:] + back_dev:
        pl.semaphore_signal(barrier, inc=1, device_id=other, device_id_type=MESH)

    def cols(q):
        return pl.ds(q * piece, piece)

    small = [
        pltpu.make_async_copy(route_hbm, route_v, load_sem.at[0]),
        pltpu.make_async_copy(gate_hbm, gate_v, load_sem.at[1]),
    ]
    row_loads = [
        [
            pltpu.make_async_copy(src.at[:, cols(q)], dst.at[:, cols(q)],
                                  load_sem.at[5 + kind * PIECES + q])
            for q in range(PIECES)
        ]
        for kind, (src, dst) in enumerate(((x_hbm, x_v), (g_hbm, g_v)))
    ]
    weights = [
        pltpu.make_async_copy(wg_hbm, wgu.at[:, :, pl.ds(0, block)], load_sem.at[2]),
        pltpu.make_async_copy(wu_hbm, wgu.at[:, :, pl.ds(block, block)], load_sem.at[3]),
        pltpu.make_async_copy(wd_hbm, wd_v, load_sem.at[4]),
    ]
    for copy in small + row_loads[0] + row_loads[1]:
        copy.start()
    for copy in small:
        copy.wait()
    pick, coef = pick_slots(route_v[...], gate_v[...])
    pick_mat = pick.astype(jnp.bfloat16)

    for kind in range(2):
        source = x_v if kind == 0 else g_v
        for q in range(PIECES):
            row_loads[kind][q].wait()
            rows = jnp.dot(
                pick_mat, source[:, q * piece:(q + 1) * piece], preferred_element_type=jnp.float32
            )
            scaled = rows if kind == 0 else rows * coef
            for i in range(slots):
                staged[i, kind * PIECES + q:kind * PIECES + q + 1, :] = scaled[i:i + 1, :]
                if kind == 1:
                    plain[i, q:q + 1, :] = rows[i:i + 1, :]

    def index(spot, k):
        return (k % 2) * 8 + spot * 2 + lax.rem(z // 2 + k // 2, 2)

    own = index(xy, 0)
    for i in range(slots):
        gath[own, i] = staged[i].astype(jnp.bfloat16)
    plain_in[0] = plain[...].astype(jnp.bfloat16)
    for copy in weights:
        copy.start()
    pl.semaphore_wait(barrier, 9)

    def remote(src, dst, send, recv, to):
        return pltpu.make_async_remote_copy(
            src_ref=src, dst_ref=dst, send_sem=send, recv_sem=recv, device_id=to,
            device_id_type=MESH,
        )

    sent = []

    def start(copy):
        copy.start()
        sent.append(copy)
        return copy

    for k in (2, 1, 3):
        start(remote(gath.at[own], gath.at[(k % 2) * 8 + xy * 2 + z // 2],
                     z_send.at[k], z_recv.at[k], z_dev[k]))

    def halves(k):
        if k % 2 == 1:
            return (pl.ds(0, slots),)
        cut = 3 if k == 0 else 2
        return (pl.ds(0, cut), pl.ds(cut, slots - cut))

    def slab(spot, k, half):
        return gath.at[index(spot, k), halves(k)[half]]

    def over(axis, k, half):
        ref = slab(xy, k, half)
        return remote(ref, ref, xy_send.at[axis, k, half], xy_recv.at[axis, k, half],
                      x_dev if axis == 0 else y_dev)

    def to_plane(k):
        if k % 2 == 1:
            start(over(0, k, 0))
            start(over(1, k, 0))
        else:
            start(over(0, k, 0))
            start(over(1, k, 1))
            start(over(0, k, 1))
            start(over(1, k, 0))

    def arrived(axis, k, half):
        ref = slab(at_x if axis == 0 else at_y, k, half)
        remote(ref, ref, xy_send.at[axis, k, half], xy_recv.at[axis, k, half], x_dev).wait_recv()

    def to_corner(k):
        arrived(0, k, 0)
        ref = slab(at_x, k, 0)
        start(remote(ref, ref, d_send.at[k // 2, 0], d_recv.at[k // 2, 0], y_dev))
        arrived(1, k, 1)
        ref = slab(at_y, k, 1)
        start(remote(ref, ref, d_send.at[k // 2, 1], d_recv.at[k // 2, 1], x_dev))

    def corner_arrived(k):
        for half in range(2):
            ref = slab(at_d, k, half)
            remote(ref, ref, d_send.at[k // 2, half], d_recv.at[k // 2, half], y_dev).wait_recv()

    def z_arrived(k):
        ref = gath.at[index(xy, k)]
        remote(ref, ref, z_send.at[k], z_recv.at[k], z_dev[k]).wait_recv()

    def corner_over_z(k):
        source = index(at_d, k)
        return remote(gath.at[source], gath.at[8 + source], dz_send.at[k // 2],
                      dz_recv.at[k // 2], z_dev[1])

    to_plane(0)
    plain_copy = start(remote(plain_in.at[0], plain_in.at[1], p_send, p_recv, back_dev[0]))
    z_arrived(2)
    to_plane(2)
    to_corner(0)
    to_corner(2)
    z_arrived(1)
    to_plane(1)
    corner_arrived(0)
    start(corner_over_z(0))
    z_arrived(3)
    to_plane(3)
    corner_arrived(2)
    start(corner_over_z(2))

    group_rows = slots * 8
    to_rows = swap_order(8, 2 * PIECES)
    to_units = swap_order(PIECES, 8)
    chunks = ((0, 3), (3, slots - 3))

    def compute(r):
        for i in range(slots):
            packed = gath[r * 8:(r + 1) * 8, i].reshape(8 * 2 * PIECES, piece)
            ordered = jnp.dot(to_rows, packed, preferred_element_type=jnp.float32)
            at = r * group_rows + i * 8
            for q in range(PIECES):
                xf[q, at:at + 8, :] = ordered[q * 8:(q + 1) * 8].astype(jnp.bfloat16)
                gf[q, at:at + 8, :] = ordered[
                    (PIECES + q) * 8:(PIECES + q + 1) * 8
                ].astype(jnp.bfloat16)
        mine = slice(r * group_rows, (r + 1) * group_rows)
        pre = jnp.zeros((group_rows, 2 * block), jnp.float32)
        back = jnp.zeros((group_rows, block), jnp.float32)
        for q in range(PIECES):
            pre = pre + jnp.dot(xf[q, mine, :], wgu[q], preferred_element_type=jnp.float32)
            back = back + lax.dot_general(
                gf[q, mine, :], wd_v[:, q * piece:(q + 1) * piece], CONTRACT_LAST,
                preferred_element_type=jnp.float32,
            )
        hidden, grad_gate, grad_up = hidden_grads(pre[:, :block], pre[:, block:], back)
        grad_both = jnp.concatenate(
            [grad_gate.astype(jnp.bfloat16), grad_up.astype(jnp.bfloat16)], axis=1
        )
        return hidden, grad_both

    def diagonal(r, c, half):
        lo, count = chunks[c]
        at = pl.ds(lo, count)
        return remote(part.at[r, at, at_d, half], diag_in.at[r, at, half],
                      s1_send.at[r, c, half], s1_recv.at[r, c, half],
                      y_dev if half == 0 else x_dev)

    def direct(r, c, half):
        lo, count = chunks[c]
        at = pl.ds(lo, count)
        if half == 1:
            return remote(part.at[r, at, at_x, 1], in_x.at[r, at, 1], s1_send.at[r, c, 2],
                          s1_recv.at[r, c, 2], x_dev)
        return remote(part.at[r, at, at_y, 0], in_y.at[r, at, 0], s1_send.at[r, c, 3],
                      s1_recv.at[r, c, 3], y_dev)

    def passed(r, c, half):
        lo, count = chunks[c]
        at = pl.ds(lo, count)
        if half == 0:
            return remote(fwd_x.at[r, at], in_x.at[r, at, 0], s2_send.at[r, c, 0],
                          s2_recv.at[r, c, 0], x_dev)
        return remote(fwd_y.at[r, at], in_y.at[r, at, 1], s2_send.at[r, c, 1],
                      s2_recv.at[r, c, 1], y_dev)

    def homeward(r, c, k):
        lo, count = chunks[c]
        at = pl.ds(lo, count)
        return remote(zsum.at[r, at, lax.rem(z // 2 + k // 2, 2)], in_z.at[k, at],
                      s3_send.at[c, k], s3_recv.at[c, k], back_dev[k])

    def send_shares(r, grad_both):
        for q in range(PIECES):
            share = lax.dot_general(
                grad_both, wgu[q], CONTRACT_LAST, preferred_element_type=jnp.float32
            ).astype(jnp.bfloat16)
            for i in range(slots):
                pfull[r, i, q * 8:(q + 1) * 8, :] = share[i * 8:(i + 1) * 8]
        for c, (lo, count) in enumerate(chunks):
            for i in range(lo, lo + count):
                units = jnp.dot(to_units, pfull[r, i], preferred_element_type=jnp.float32)
                part[r, i] = units.reshape(4, 2, PIECES, piece).astype(jnp.bfloat16)
            for half in range(2):
                start(diagonal(r, c, half))
        for c in range(2):
            for half in range(2):
                start(direct(r, c, half))

    def pass_on(r):
        for c, (lo, count) in enumerate(chunks):
            for half in range(2):
                diagonal(r, c, half).wait_recv()
                spot, out = (at_x, fwd_x) if half == 0 else (at_y, fwd_y)
                for i in range(lo, lo + count):
                    out[r, i] = (
                        part[r, i, spot, half].astype(jnp.float32)
                        + diag_in[r, i, half].astype(jnp.float32)
                    ).astype(jnp.bfloat16)
                start(passed(r, c, half))

    def send_home(r):
        for c, (lo, count) in enumerate(chunks):
            for half in range(2):
                direct(r, c, half).wait_recv()
                passed(r, c, half).wait_recv()
            for i in range(lo, lo + count):
                zsum[r, i] = (
                    part[r, i, xy].astype(jnp.float32) + in_x[r, i].astype(jnp.float32)
                    + in_y[r, i].astype(jnp.float32)
                ).astype(jnp.bfloat16)
            for k in (r + 2, r):
                start(homeward(r, c, k))

    arrived(0, 0, 1)
    arrived(1, 0, 0)
    arrived(0, 2, 1)
    arrived(1, 2, 0)
    for copy in weights:
        copy.wait()
    hidden_a, grad_both = compute(0)
    send_shares(0, grad_both)
    for k in (1, 3):
        arrived(0, k, 0)
        arrived(1, k, 0)
    for k in (0, 2):
        corner_over_z(k).wait_recv()
    hidden_b, grad_both = compute(1)
    pass_on(0)
    send_shares(1, grad_both)
    hidden_t = jnp.transpose(jnp.concatenate([hidden_a, hidden_b], axis=0)).astype(jnp.bfloat16)

    def down_piece(q):
        down_v[:, q * piece:(q + 1) * piece] = jnp.dot(
            hidden_t, gf[q], preferred_element_type=jnp.float32
        ).astype(jnp.bfloat16)

    for q in range(PIECES // 2):
        down_piece(q)
    pass_on(1)
    send_home(0)
    for q in range(PIECES // 2, PIECES):
        down_piece(q)
    down_copy = pltpu.make_async_copy(down_v, down_out, out_sem.at[0])
    down_copy.start()
    send_home(1)

    plain_copy.wait_recv()
    rows_v[slots:] = jnp.zeros((rows_v.shape[0] - slots, rows_v.shape[1]), jnp.float32)
    for c, (lo, count) in enumerate(chunks):
        for k in range(4):
            homeward(k % 2, c, k).wait_recv()
        for i in range(lo, lo + count):
            total = plain_in[1, i].astype(jnp.float32)
            for k in range(4):
                total = total + in_z[k, i].astype(jnp.float32)
            for q in range(PIECES):
                rows_v[i:i + 1, q * piece:(q + 1) * piece] = total[q:q + 1, :]
    rows_copy = pltpu.make_async_copy(rows_v, rows_out, out_sem.at[1])
    rows_copy.start()
    for copy in sent:
        copy.wait_send()
    down_copy.wait()
    rows_copy.wait()


def group_work(inputs, grads, gate_cols, up_cols, down_rows, route, gate):
    tok, width = inputs.shape
    block = gate_cols.shape[1]
    piece = width // PIECES
    bf16 = jnp.bfloat16
    whole = pl.BlockSpec(memory_space=pl.ANY)
    dma = pltpu.SemaphoreType.DMA
    pairs = pltpu.VMEM((2, CAP, 2, PIECES, piece), bf16)
    singles = pltpu.VMEM((2, CAP, PIECES, piece), bf16)
    return pl.pallas_call(
        group_kernel,
        out_shape=(
            jax.ShapeDtypeStruct((8, width), jnp.float32),
            jax.ShapeDtypeStruct((block, width), bf16),
        ),
        in_specs=[whole] * 7,
        out_specs=(whole, whole),
        scratch_shapes=[
            pltpu.VMEM(route.shape[::-1], jnp.int32),
            pltpu.VMEM(gate.shape[::-1], jnp.float32),
            pltpu.VMEM((tok, width), bf16),
            pltpu.VMEM((tok, width), bf16),
            pltpu.VMEM((PIECES, piece, 2 * block), bf16),
            pltpu.VMEM((block, width), bf16),
            pltpu.VMEM((CAP, 2 * PIECES, piece), jnp.float32),
            pltpu.VMEM((CAP, PIECES, piece), jnp.float32),
            singles,
            pltpu.VMEM((SHARDS, CAP, 2 * PIECES, piece), bf16),
            pltpu.VMEM((PIECES, CAP * SHARDS, piece), bf16),
            pltpu.VMEM((PIECES, CAP * SHARDS, piece), bf16),
            pltpu.VMEM((2, CAP, 8 * PIECES, piece), bf16),
            pltpu.VMEM((2, CAP, 4, 2, PIECES, piece), bf16),
            pairs,
            singles,
            singles,
            pairs,
            pairs,
            pairs,
            pltpu.VMEM((4, CAP, PIECES, piece), bf16),
            pltpu.VMEM((block, width), bf16),
            pltpu.VMEM((8, width), jnp.float32),
            dma((5 + 2 * PIECES,)), dma((2,)), dma((4,)), dma((4,)), dma((2, 4, 2)),
            dma((2, 4, 2)), dma((2, 2)), dma((2, 2)), dma((2,)), dma((2,)), dma, dma,
            dma((2, 2, 4)), dma((2, 2, 4)), dma((2, 2, 2)), dma((2, 2, 2)),
            dma((2, 4)), dma((2, 4)),
        ],
        compiler_params=pltpu.CompilerParams(
            collective_id=0, has_side_effects=True, vmem_limit_bytes=60 * 2**20
        ),
        cost_estimate=pl.CostEstimate(
            flops=12 * CAP * SHARDS * width * block, bytes_accessed=14 * tok * width,
            transcendentals=CAP * SHARDS * block,
        ),
        name="relay_group",
    )(
        inputs, grads, gate_cols.reshape(PIECES, piece, block),
        up_cols.reshape(PIECES, piece, block), down_rows, route.T, gate.T,
    )


def finish_kernel(route_hbm, rows_hbm, grads_hbm, down_hbm, handed_out, down_out,
                  route_v, rows_v, grads_v, done_v, sem, down_sem):
    piece = grads_v.shape[1] // PIECES

    def cols(q):
        return pl.ds(q * piece, piece)

    first = [
        pltpu.make_async_copy(route_hbm, route_v, sem.at[0]),
        pltpu.make_async_copy(rows_hbm, rows_v, sem.at[1]),
    ]
    loads = [
        pltpu.make_async_copy(grads_hbm.at[:, cols(q)], grads_v.at[:, cols(q)], sem.at[2 + q])
        for q in range(PIECES)
    ]
    stores = [
        pltpu.make_async_copy(done_v.at[:, cols(q)], handed_out.at[:, cols(q)],
                              sem.at[2 + PIECES + q])
        for q in range(PIECES)
    ]
    downs = [
        pltpu.make_async_copy(down_hbm.at[:, cols(q)], down_out.at[:, cols(q)], down_sem.at[q])
        for q in range(PIECES)
    ]
    for copy in first + loads + downs:
        copy.start()
    for copy in first:
        copy.wait()
    pick, _ = pick_slots(route_v[...], None)
    named = jnp.transpose(pick)
    changed = jnp.sum(named, axis=1, keepdims=True) > 0.0
    named = named.astype(jnp.bfloat16)
    for q in range(PIECES):
        at = slice(q * piece, (q + 1) * piece)
        placed = jnp.dot(
            named, rows_v[:, at].astype(jnp.bfloat16), preferred_element_type=jnp.float32
        )
        loads[q].wait()
        done_v[:, at] = jnp.where(changed, placed, grads_v[:, at].astype(jnp.float32)).astype(
            jnp.bfloat16
        )
        stores[q].start()
    for copy in stores + downs:
        copy.wait()


def finish(route, rows, grads, down):
    whole = pl.BlockSpec(memory_space=pl.ANY)
    like = jax.ShapeDtypeStruct(grads.shape, grads.dtype)
    return pl.pallas_call(
        finish_kernel,
        out_shape=(like, jax.ShapeDtypeStruct(down.shape, down.dtype)),
        in_specs=[whole] * 4,
        out_specs=(whole, whole),
        scratch_shapes=[
            pltpu.VMEM(route.shape[::-1], jnp.int32),
            pltpu.VMEM(rows.shape, rows.dtype),
            pltpu.VMEM(grads.shape, grads.dtype),
            pltpu.VMEM(grads.shape, grads.dtype),
            pltpu.SemaphoreType.DMA((2 + 2 * PIECES,)),
            pltpu.SemaphoreType.DMA((PIECES,)),
        ],
        compiler_params=pltpu.CompilerParams(vmem_limit_bytes=60 * 2**20),
        cost_estimate=pl.CostEstimate(
            flops=16 * grads.size, bytes_accessed=8 * grads.size, transcendentals=0
        ),
        name="relay_finish",
    )(route.T, rows, grads, down)


def plain_work(rows, gate_cols, up_cols, down_rows):
    width = lax.axis_size("expert")
    live = width // SHARDS
    across = [[g * SHARDS + j for g in range(live)] for j in range(SHARDS)]
    within = [[g * SHARDS + j for j in range(SHARDS)] for g in range(live)]
    kinds, count, model_width = rows.shape
    if live > 1:
        rows = lax.all_to_all(
            rows, "expert", split_axis=1, concat_axis=1, tiled=True, axis_index_groups=across
        )
    got = lax.all_gather(rows, "expert", axis=1, tiled=True, axis_index_groups=within)
    flat_in, flat_grad = got[0], got[1]
    gate_pre = jnp.dot(flat_in, gate_cols, preferred_element_type=jnp.float32)
    up_pre = jnp.dot(flat_in, up_cols, preferred_element_type=jnp.float32)
    back = lax.dot_general(flat_grad, down_rows, CONTRACT_LAST, preferred_element_type=jnp.float32)
    hidden, grad_gate, grad_up = hidden_grads(gate_pre, up_pre, back)
    share = lax.dot_general(
        grad_gate.astype(jnp.bfloat16), gate_cols, CONTRACT_LAST,
        preferred_element_type=jnp.float32,
    ) + lax.dot_general(
        grad_up.astype(jnp.bfloat16), up_cols, CONTRACT_LAST, preferred_element_type=jnp.float32
    )
    summed = lax.psum_scatter(
        share.astype(jnp.bfloat16), "expert", scatter_dimension=0, tiled=True,
        axis_index_groups=within,
    )
    if live > 1:
        summed = lax.all_to_all(
            summed, "expert", split_axis=0, concat_axis=0, tiled=True, axis_index_groups=across
        )
    down_part = lax.dot_general(
        hidden.astype(jnp.bfloat16), flat_grad, ROWS_FIRST, preferred_element_type=jnp.float32
    ).astype(jnp.bfloat16)
    return summed, down_part


def slot_picks(route, gate, live):
    hit = route[:, :, None] == jnp.arange(live, dtype=jnp.int32)
    member = jnp.sum(hit.astype(jnp.int32), axis=1)
    weight = jnp.sum(jnp.where(hit, gate[:, :, None], 0.0), axis=1)
    position = jnp.cumsum(member, axis=0) - member
    pick = (member[:, :, None] == 1) & (
        position[:, :, None] == jnp.arange(CAP, dtype=jnp.int32)
    )
    return member, weight, pick


def other_core(value):
    return lax.ppermute(value, "pipe", [(0, 1), (1, 0)])


def body(section_inputs, output_grads, w_gate, w_up, w_down, route_ids, route_gates):
    inputs, grads, route, gate = section_inputs[0], output_grads[0], route_ids[0], route_gates[0]
    gate_cols, up_cols, down_rows = w_gate[0], w_up[0], w_down[0]
    tok_rows = inputs.shape[0]
    live = lax.axis_size("expert") // SHARDS
    if live == 1:
        grads_behind = other_core(grads)
        route_behind = other_core(route)
        rows, down_part = group_work(inputs, grads, gate_cols, up_cols, down_rows, route, gate)
        handed, down_part = finish(route_behind, rows, grads_behind, down_part)
        return handed[None], down_part[None]
    _, weight, pick = slot_picks(route, gate, live)
    pick_mat = pick.astype(jnp.bfloat16).reshape(tok_rows, live * CAP)
    rows_in = lax.dot_general(pick_mat, inputs, ROWS_FIRST, preferred_element_type=jnp.float32)
    chosen = lax.dot_general(pick_mat, grads, ROWS_FIRST, preferred_element_type=jnp.float32)
    slot_gate = jnp.sum(pick.astype(jnp.float32) * weight[:, :, None], axis=0).reshape(-1, 1)
    rows = jnp.stack([rows_in.astype(jnp.bfloat16), (chosen * slot_gate).astype(jnp.bfloat16)])
    summed, down_part = plain_work(rows, gate_cols, up_cols, down_rows)
    branch = jnp.dot(pick_mat, summed, preferred_element_type=jnp.float32)
    input_grad = (grads.astype(jnp.float32) + branch).astype(jnp.bfloat16)
    return other_core(input_grad)[None], down_part[None]


def solution(mesh):
    return jax.shard_map(
        body,
        mesh=mesh,
        in_specs=(
            P("pipe", "expert", None),
            P("pipe", "expert", None),
            P("pipe", None, "expert"),
            P("pipe", None, "expert"),
            P("pipe", "expert", None),
            P("pipe", "expert", None),
            P("pipe", "expert", None),
        ),
        out_specs=(P("pipe", "expert", None), P("pipe", "expert", None)),
        check_vma=False,
    )
```

```python
import jax
import jax.numpy as jnp
from jax import lax
from jax.experimental import pallas as pl
from jax.experimental.pallas import tpu as pltpu
from jax.sharding import PartitionSpec as P

SHARDS = 16
CAP = 5
PIECES = 8
MESH = pl.DeviceIdType.MESH
CONTRACT_LAST = (((1,), (1,)), ((), ()))
ROWS_FIRST = (((0,), (0,)), ((), ()))


def hidden_grads(gate_pre, up_pre, back_hidden):
    sigma = jax.nn.sigmoid(gate_pre)
    silu_gate = gate_pre * sigma
    hidden = silu_gate * up_pre
    grad_gate = back_hidden * up_pre * sigma * (1.0 + gate_pre * (1.0 - sigma))
    grad_up = back_hidden * silu_gate
    return hidden, grad_gate, grad_up


def flip(z, k):
    if k == 0:
        return z
    if k == 1:
        return z + 1 - 2 * lax.rem(z, 2)
    if k == 2:
        return lax.rem(z + 2, 4)
    return 3 - z


def pick_slots(route, gate):
    tok = route.shape[1]
    hit = route == 0
    member = jnp.sum(jnp.where(hit, 1.0, 0.0), axis=0, keepdims=True)
    earlier = lax.broadcasted_iota(jnp.int32, (tok, tok), 0) < lax.broadcasted_iota(
        jnp.int32, (tok, tok), 1
    )
    member8 = jnp.broadcast_to(member, (8, tok))
    position = jnp.dot(
        member8.astype(jnp.bfloat16),
        jnp.where(earlier, 1.0, 0.0).astype(jnp.bfloat16),
        preferred_element_type=jnp.float32,
    )
    slot = lax.broadcasted_iota(jnp.int32, (8, tok), 0).astype(jnp.float32)
    pick = jnp.where((member8 == 1.0) & (position == slot), 1.0, 0.0)
    weight = jnp.sum(jnp.where(hit, gate, 0.0), axis=0, keepdims=True)
    return pick, jnp.sum(pick * weight, axis=1, keepdims=True)


def swap_order(outer, inner):
    size = outer * inner
    r = lax.broadcasted_iota(jnp.int32, (size, size), 0)
    c = lax.broadcasted_iota(jnp.int32, (size, size), 1)
    source = lax.rem(r, outer) * inner + r // outer
    return jnp.where(c == source, 1.0, 0.0).astype(jnp.bfloat16)


def group_kernel(
    x_hbm, g_hbm, wg_hbm, wu_hbm, wd_hbm, route_hbm, gate_hbm,
    rows_out, down_out,
    route_v, gate_v, pick_v, x_v, g_v, wgu, wd_v, staged, plain, plain_in, gath, xf, gf, pfull, part,
    diag_in, fwd_x, fwd_y, in_x, in_y, zsum, in_z, down_v, rows_v,
    load_sem, out_sem, z_send, z_recv, xy_send, xy_recv, d_send, d_recv, dz_send, dz_recv,
    p_send, p_recv, t_send, t_recv, s1_send, s1_recv, s2_send, s2_recv, s3_send, s3_recv,
):
    slots, piece = staged.shape[0], staged.shape[2]
    block = wd_v.shape[0]
    pipe = lax.axis_index("pipe")
    me = lax.axis_index("expert")
    base = (me // SHARDS) * SHARDS
    local = lax.rem(me, SHARDS)
    z = local // 4
    xy = lax.rem(local, 4)
    y, x = xy // 2, lax.rem(xy, 2)
    at_x, at_y, at_d = y * 2 + 1 - x, (1 - y) * 2 + x, 3 - xy

    def device(p, zz, spot):
        return {"pipe": p, "expert": base + zz * 4 + spot}

    x_dev, y_dev = device(pipe, z, at_x), device(pipe, z, at_y)
    z_dev = [device(pipe, flip(z, k), xy) for k in range(4)]
    back_dev = [device(1 - pipe, flip(z, k), xy) for k in range(4)]

    barrier = pltpu.get_barrier_semaphore()
    for other in [x_dev, y_dev] + z_dev[1:] + back_dev:
        pl.semaphore_signal(barrier, inc=1, device_id=other, device_id_type=MESH)

    def cols(q):
        return pl.ds(q * piece, piece)

    small = [
        pltpu.make_async_copy(route_hbm, route_v, load_sem.at[0]),
        pltpu.make_async_copy(gate_hbm, gate_v, load_sem.at[1]),
    ]
    row_loads = [
        [
            pltpu.make_async_copy(src.at[:, cols(q)], dst.at[:, cols(q)],
                                  load_sem.at[5 + kind * PIECES + q])
            for q in range(PIECES)
        ]
        for kind, (src, dst) in enumerate(((x_hbm, x_v), (g_hbm, g_v)))
    ]
    weights = [
        pltpu.make_async_copy(wg_hbm, wgu.at[:, :, pl.ds(0, block)], load_sem.at[2]),
        pltpu.make_async_copy(wu_hbm, wgu.at[:, :, pl.ds(block, block)], load_sem.at[3]),
        pltpu.make_async_copy(wd_hbm, wd_v, load_sem.at[4]),
    ]
    for copy in small + row_loads[0] + row_loads[1]:
        copy.start()
    for copy in small:
        copy.wait()
    pick, coef = pick_slots(route_v[...], gate_v[...])
    pick_v[...] = pick
    pick_mat = pick.astype(jnp.bfloat16)

    for kind in range(2):
        source = x_v if kind == 0 else g_v
        for q in range(PIECES):
            row_loads[kind][q].wait()
            rows = jnp.dot(
                pick_mat, source[:, q * piece:(q + 1) * piece], preferred_element_type=jnp.float32
            )
            scaled = rows if kind == 0 else rows * coef
            for i in range(slots):
                staged[i, kind * PIECES + q:kind * PIECES + q + 1, :] = scaled[i:i + 1, :]
                if kind == 1:
                    plain[i, q:q + 1, :] = rows[i:i + 1, :]

    def index(spot, k):
        return (k % 2) * 8 + spot * 2 + lax.rem(z // 2 + k // 2, 2)

    own = index(xy, 0)
    for i in range(slots):
        gath[own, i] = staged[i].astype(jnp.bfloat16)
    plain_in[0] = plain[...].astype(jnp.bfloat16)
    for copy in weights:
        copy.start()
    pl.semaphore_wait(barrier, 9)

    def remote(src, dst, send, recv, to):
        return pltpu.make_async_remote_copy(
            src_ref=src, dst_ref=dst, send_sem=send, recv_sem=recv, device_id=to,
            device_id_type=MESH,
        )

    sent = []

    def start(copy):
        copy.start()
        sent.append(copy)
        return copy

    for k in (2, 1, 3):
        start(remote(gath.at[own], gath.at[(k % 2) * 8 + xy * 2 + z // 2],
                     z_send.at[k], z_recv.at[k], z_dev[k]))

    def halves(k):
        if k % 2 == 1:
            return (pl.ds(0, slots),)
        cut = 3 if k == 0 else 2
        return (pl.ds(0, cut), pl.ds(cut, slots - cut))

    def slab(spot, k, half):
        return gath.at[index(spot, k), halves(k)[half]]

    def over(axis, k, half):
        ref = slab(xy, k, half)
        return remote(ref, ref, xy_send.at[axis, k, half], xy_recv.at[axis, k, half],
                      x_dev if axis == 0 else y_dev)

    def to_plane(k):
        if k % 2 == 1:
            start(over(0, k, 0))
            start(over(1, k, 0))
        else:
            start(over(0, k, 0))
            start(over(1, k, 1))
            start(over(0, k, 1))
            start(over(1, k, 0))

    def arrived(axis, k, half):
        ref = slab(at_x if axis == 0 else at_y, k, half)
        remote(ref, ref, xy_send.at[axis, k, half], xy_recv.at[axis, k, half], x_dev).wait_recv()

    def to_corner(k):
        arrived(0, k, 0)
        ref = slab(at_x, k, 0)
        start(remote(ref, ref, d_send.at[k // 2, 0], d_recv.at[k // 2, 0], y_dev))
        arrived(1, k, 1)
        ref = slab(at_y, k, 1)
        start(remote(ref, ref, d_send.at[k // 2, 1], d_recv.at[k // 2, 1], x_dev))

    def corner_arrived(k):
        for half in range(2):
            ref = slab(at_d, k, half)
            remote(ref, ref, d_send.at[k // 2, half], d_recv.at[k // 2, half], y_dev).wait_recv()

    def z_arrived(k):
        ref = gath.at[index(xy, k)]
        remote(ref, ref, z_send.at[k], z_recv.at[k], z_dev[k]).wait_recv()

    def corner_over_z(k):
        source = index(at_d, k)
        return remote(gath.at[source], gath.at[8 + source], dz_send.at[k // 2],
                      dz_recv.at[k // 2], z_dev[1])

    to_plane(0)
    plain_copy = start(remote(plain_in.at[0], plain_in.at[1], p_send, p_recv, back_dev[0]))
    width = x_v.shape[1]
    pick_copy = start(
        remote(pick_v, rows_v.at[:, pl.ds(width, pick_v.shape[1])], t_send, t_recv, back_dev[0])
    )
    z_arrived(2)
    to_plane(2)
    to_corner(0)
    to_corner(2)
    z_arrived(1)
    to_plane(1)
    corner_arrived(0)
    start(corner_over_z(0))
    z_arrived(3)
    to_plane(3)
    corner_arrived(2)
    start(corner_over_z(2))

    group_rows = slots * 8
    to_rows = swap_order(8, 2 * PIECES)
    to_units = swap_order(PIECES, 8)
    chunks = ((0, 3), (3, slots - 3))

    def compute(r):
        for i in range(slots):
            packed = gath[r * 8:(r + 1) * 8, i].reshape(8 * 2 * PIECES, piece)
            ordered = jnp.dot(to_rows, packed, preferred_element_type=jnp.float32)
            at = r * group_rows + i * 8
            for q in range(PIECES):
                xf[q, at:at + 8, :] = ordered[q * 8:(q + 1) * 8].astype(jnp.bfloat16)
                gf[q, at:at + 8, :] = ordered[
                    (PIECES + q) * 8:(PIECES + q + 1) * 8
                ].astype(jnp.bfloat16)
        mine = slice(r * group_rows, (r + 1) * group_rows)
        pre = jnp.zeros((group_rows, 2 * block), jnp.float32)
        back = jnp.zeros((group_rows, block), jnp.float32)
        for q in range(PIECES):
            pre = pre + jnp.dot(xf[q, mine, :], wgu[q], preferred_element_type=jnp.float32)
            back = back + lax.dot_general(
                gf[q, mine, :], wd_v[:, q * piece:(q + 1) * piece], CONTRACT_LAST,
                preferred_element_type=jnp.float32,
            )
        hidden, grad_gate, grad_up = hidden_grads(pre[:, :block], pre[:, block:], back)
        grad_both = jnp.concatenate(
            [grad_gate.astype(jnp.bfloat16), grad_up.astype(jnp.bfloat16)], axis=1
        )
        return hidden, grad_both

    def diagonal(r, c, half):
        lo, count = chunks[c]
        at = pl.ds(lo, count)
        return remote(part.at[r, at, at_d, half], diag_in.at[r, at, half],
                      s1_send.at[r, c, half], s1_recv.at[r, c, half],
                      y_dev if half == 0 else x_dev)

    def direct(r, c, half):
        lo, count = chunks[c]
        at = pl.ds(lo, count)
        if half == 1:
            return remote(part.at[r, at, at_x, 1], in_x.at[r, at, 1], s1_send.at[r, c, 2],
                          s1_recv.at[r, c, 2], x_dev)
        return remote(part.at[r, at, at_y, 0], in_y.at[r, at, 0], s1_send.at[r, c, 3],
                      s1_recv.at[r, c, 3], y_dev)

    def passed(r, c, half):
        lo, count = chunks[c]
        at = pl.ds(lo, count)
        if half == 0:
            return remote(fwd_x.at[r, at], in_x.at[r, at, 0], s2_send.at[r, c, 0],
                          s2_recv.at[r, c, 0], x_dev)
        return remote(fwd_y.at[r, at], in_y.at[r, at, 1], s2_send.at[r, c, 1],
                      s2_recv.at[r, c, 1], y_dev)

    def homeward(r, c, k):
        lo, count = chunks[c]
        at = pl.ds(lo, count)
        return remote(zsum.at[r, at, lax.rem(z // 2 + k // 2, 2)], in_z.at[k, at],
                      s3_send.at[c, k], s3_recv.at[c, k], back_dev[k])

    def send_shares(r, grad_both):
        for q in range(PIECES):
            share = lax.dot_general(
                grad_both, wgu[q], CONTRACT_LAST, preferred_element_type=jnp.float32
            ).astype(jnp.bfloat16)
            for i in range(slots):
                pfull[r, i, q * 8:(q + 1) * 8, :] = share[i * 8:(i + 1) * 8]
        for c, (lo, count) in enumerate(chunks):
            for i in range(lo, lo + count):
                units = jnp.dot(to_units, pfull[r, i], preferred_element_type=jnp.float32)
                part[r, i] = units.reshape(4, 2, PIECES, piece).astype(jnp.bfloat16)
            for half in range(2):
                start(diagonal(r, c, half))
        for c in range(2):
            for half in range(2):
                start(direct(r, c, half))

    def pass_on(r):
        for c, (lo, count) in enumerate(chunks):
            for half in range(2):
                diagonal(r, c, half).wait_recv()
                spot, out = (at_x, fwd_x) if half == 0 else (at_y, fwd_y)
                for i in range(lo, lo + count):
                    out[r, i] = (
                        part[r, i, spot, half].astype(jnp.float32)
                        + diag_in[r, i, half].astype(jnp.float32)
                    ).astype(jnp.bfloat16)
                start(passed(r, c, half))

    def send_home(r):
        for c, (lo, count) in enumerate(chunks):
            for half in range(2):
                direct(r, c, half).wait_recv()
                passed(r, c, half).wait_recv()
            for i in range(lo, lo + count):
                zsum[r, i] = (
                    part[r, i, xy].astype(jnp.float32) + in_x[r, i].astype(jnp.float32)
                    + in_y[r, i].astype(jnp.float32)
                ).astype(jnp.bfloat16)
            for k in (r + 2, r):
                start(homeward(r, c, k))

    arrived(0, 0, 1)
    arrived(1, 0, 0)
    arrived(0, 2, 1)
    arrived(1, 2, 0)
    for copy in weights:
        copy.wait()
    hidden_a, grad_both = compute(0)
    send_shares(0, grad_both)
    for k in (1, 3):
        arrived(0, k, 0)
        arrived(1, k, 0)
    for k in (0, 2):
        corner_over_z(k).wait_recv()
    hidden_b, grad_both = compute(1)
    pass_on(0)
    send_shares(1, grad_both)
    hidden_t = jnp.transpose(jnp.concatenate([hidden_a, hidden_b], axis=0)).astype(jnp.bfloat16)

    def down_piece(q):
        down_v[:, q * piece:(q + 1) * piece] = jnp.dot(
            hidden_t, gf[q], preferred_element_type=jnp.float32
        ).astype(jnp.bfloat16)

    send_home(0)
    for q in range(PIECES // 2):
        down_piece(q)
    pass_on(1)
    for q in range(PIECES // 2, PIECES):
        down_piece(q)
    down_copy = pltpu.make_async_copy(down_v, down_out, out_sem.at[0])
    down_copy.start()
    send_home(1)

    plain_copy.wait_recv()
    pick_copy.wait_recv()
    rows_v[slots:, :width] = jnp.zeros((rows_v.shape[0] - slots, width), jnp.float32)
    for c, (lo, count) in enumerate(chunks):
        for k in range(4):
            homeward(k % 2, c, k).wait_recv()
        for i in range(lo, lo + count):
            total = plain_in[1, i].astype(jnp.float32)
            for k in range(4):
                total = total + in_z[k, i].astype(jnp.float32)
            for q in range(PIECES):
                rows_v[i:i + 1, q * piece:(q + 1) * piece] = total[q:q + 1, :]
    rows_copy = pltpu.make_async_copy(rows_v, rows_out, out_sem.at[1])
    rows_copy.start()
    for copy in sent:
        copy.wait_send()
    down_copy.wait()
    rows_copy.wait()


def group_work(inputs, grads, gate_cols, up_cols, down_rows, route, gate):
    tok, width = inputs.shape
    block = gate_cols.shape[1]
    piece = width // PIECES
    bf16 = jnp.bfloat16
    whole = pl.BlockSpec(memory_space=pl.ANY)
    dma = pltpu.SemaphoreType.DMA
    pairs = pltpu.VMEM((2, CAP, 2, PIECES, piece), bf16)
    singles = pltpu.VMEM((2, CAP, PIECES, piece), bf16)
    return pl.pallas_call(
        group_kernel,
        out_shape=(
            jax.ShapeDtypeStruct((8, width + tok), jnp.float32),
            jax.ShapeDtypeStruct((block, width), bf16),
        ),
        in_specs=[whole] * 7,
        out_specs=(whole, whole),
        scratch_shapes=[
            pltpu.VMEM(route.shape[::-1], jnp.int32),
            pltpu.VMEM(gate.shape[::-1], jnp.float32),
            pltpu.VMEM((8, tok), jnp.float32),
            pltpu.VMEM((tok, width), bf16),
            pltpu.VMEM((tok, width), bf16),
            pltpu.VMEM((PIECES, piece, 2 * block), bf16),
            pltpu.VMEM((block, width), bf16),
            pltpu.VMEM((CAP, 2 * PIECES, piece), jnp.float32),
            pltpu.VMEM((CAP, PIECES, piece), jnp.float32),
            singles,
            pltpu.VMEM((SHARDS, CAP, 2 * PIECES, piece), bf16),
            pltpu.VMEM((PIECES, CAP * SHARDS, piece), bf16),
            pltpu.VMEM((PIECES, CAP * SHARDS, piece), bf16),
            pltpu.VMEM((2, CAP, 8 * PIECES, piece), bf16),
            pltpu.VMEM((2, CAP, 4, 2, PIECES, piece), bf16),
            pairs,
            singles,
            singles,
            pairs,
            pairs,
            pairs,
            pltpu.VMEM((4, CAP, PIECES, piece), bf16),
            pltpu.VMEM((block, width), bf16),
            pltpu.VMEM((8, width + tok), jnp.float32),
            dma((5 + 2 * PIECES,)), dma((2,)), dma((4,)), dma((4,)), dma((2, 4, 2)),
            dma((2, 4, 2)), dma((2, 2)), dma((2, 2)), dma((2,)), dma((2,)), dma, dma, dma, dma,
            dma((2, 2, 4)), dma((2, 2, 4)), dma((2, 2, 2)), dma((2, 2, 2)),
            dma((2, 4)), dma((2, 4)),
        ],
        compiler_params=pltpu.CompilerParams(
            collective_id=0, has_side_effects=True, vmem_limit_bytes=60 * 2**20
        ),
        cost_estimate=pl.CostEstimate(
            flops=12 * CAP * SHARDS * width * block, bytes_accessed=14 * tok * width,
            transcendentals=CAP * SHARDS * block,
        ),
        name="relay_group",
    )(
        inputs, grads, gate_cols.reshape(PIECES, piece, block),
        up_cols.reshape(PIECES, piece, block), down_rows, route.T, gate.T,
    )


def finish_kernel(rows_hbm, grads_hbm, down_hbm, handed_out, down_out,
                  rows_v, grads_v, done_v, down_v, rows_sem, sem, down_sem):
    width = grads_v.shape[1]
    piece = width // PIECES

    def moves(source, dest, sems, first):
        return [
            pltpu.make_async_copy(source.at[:, pl.ds(q * piece, piece)],
                                  dest.at[:, pl.ds(q * piece, piece)], sems.at[first + q])
            for q in range(PIECES)
        ]

    rows_load = pltpu.make_async_copy(rows_hbm, rows_v, rows_sem)
    loads = moves(grads_hbm, grads_v, sem, 0)
    stores = moves(done_v, handed_out, sem, PIECES)
    down_loads = moves(down_hbm, down_v, down_sem, 0)
    down_stores = moves(down_v, down_out, down_sem, PIECES)
    rows_load.start()
    for q in range(PIECES):
        loads[q].start()
        down_loads[q].start()
    rows_load.wait()
    named = jnp.transpose(rows_v[:, width:])
    changed = jnp.sum(named, axis=1, keepdims=True) > 0.0
    named = named.astype(jnp.bfloat16)
    for q in range(PIECES):
        at = slice(q * piece, (q + 1) * piece)
        placed = jnp.dot(
            named, rows_v[:, at].astype(jnp.bfloat16), preferred_element_type=jnp.float32
        )
        loads[q].wait()
        done_v[:, at] = jnp.where(changed, placed, grads_v[:, at].astype(jnp.float32)).astype(
            jnp.bfloat16
        )
        stores[q].start()
        down_loads[q].wait()
        down_stores[q].start()
    for copy in stores + down_stores:
        copy.wait()


def finish(rows, grads, down):
    whole = pl.BlockSpec(memory_space=pl.ANY)
    like = jax.ShapeDtypeStruct(grads.shape, grads.dtype)
    block = pltpu.VMEM(grads.shape, grads.dtype)
    return pl.pallas_call(
        finish_kernel,
        out_shape=(like, jax.ShapeDtypeStruct(down.shape, down.dtype)),
        in_specs=[whole] * 3,
        out_specs=(whole, whole),
        scratch_shapes=[
            pltpu.VMEM(rows.shape, rows.dtype),
            block,
            block,
            pltpu.VMEM(down.shape, down.dtype),
            pltpu.SemaphoreType.DMA,
            pltpu.SemaphoreType.DMA((2 * PIECES,)),
            pltpu.SemaphoreType.DMA((2 * PIECES,)),
        ],
        compiler_params=pltpu.CompilerParams(vmem_limit_bytes=121 * 2**19),
        cost_estimate=pl.CostEstimate(
            flops=16 * grads.size, bytes_accessed=8 * grads.size, transcendentals=0
        ),
        name="relay_finish",
    )(rows, grads, down)


def plain_work(rows, gate_cols, up_cols, down_rows):
    width = lax.axis_size("expert")
    live = width // SHARDS
    across = [[g * SHARDS + j for g in range(live)] for j in range(SHARDS)]
    within = [[g * SHARDS + j for j in range(SHARDS)] for g in range(live)]
    kinds, count, model_width = rows.shape
    if live > 1:
        rows = lax.all_to_all(
            rows, "expert", split_axis=1, concat_axis=1, tiled=True, axis_index_groups=across
        )
    got = lax.all_gather(rows, "expert", axis=1, tiled=True, axis_index_groups=within)
    flat_in, flat_grad = got[0], got[1]
    gate_pre = jnp.dot(flat_in, gate_cols, preferred_element_type=jnp.float32)
    up_pre = jnp.dot(flat_in, up_cols, preferred_element_type=jnp.float32)
    back = lax.dot_general(flat_grad, down_rows, CONTRACT_LAST, preferred_element_type=jnp.float32)
    hidden, grad_gate, grad_up = hidden_grads(gate_pre, up_pre, back)
    share = lax.dot_general(
        grad_gate.astype(jnp.bfloat16), gate_cols, CONTRACT_LAST,
        preferred_element_type=jnp.float32,
    ) + lax.dot_general(
        grad_up.astype(jnp.bfloat16), up_cols, CONTRACT_LAST, preferred_element_type=jnp.float32
    )
    summed = lax.psum_scatter(
        share.astype(jnp.bfloat16), "expert", scatter_dimension=0, tiled=True,
        axis_index_groups=within,
    )
    if live > 1:
        summed = lax.all_to_all(
            summed, "expert", split_axis=0, concat_axis=0, tiled=True, axis_index_groups=across
        )
    down_part = lax.dot_general(
        hidden.astype(jnp.bfloat16), flat_grad, ROWS_FIRST, preferred_element_type=jnp.float32
    ).astype(jnp.bfloat16)
    return summed, down_part


def slot_picks(route, gate, live):
    hit = route[:, :, None] == jnp.arange(live, dtype=jnp.int32)
    member = jnp.sum(hit.astype(jnp.int32), axis=1)
    weight = jnp.sum(jnp.where(hit, gate[:, :, None], 0.0), axis=1)
    position = jnp.cumsum(member, axis=0) - member
    pick = (member[:, :, None] == 1) & (
        position[:, :, None] == jnp.arange(CAP, dtype=jnp.int32)
    )
    return member, weight, pick


def other_core(value):
    return lax.ppermute(value, "pipe", [(0, 1), (1, 0)])


def body(section_inputs, output_grads, w_gate, w_up, w_down, route_ids, route_gates):
    inputs, grads, route, gate = section_inputs[0], output_grads[0], route_ids[0], route_gates[0]
    gate_cols, up_cols, down_rows = w_gate[0], w_up[0], w_down[0]
    tok_rows = inputs.shape[0]
    live = lax.axis_size("expert") // SHARDS
    if live == 1:
        grads_behind = other_core(grads)
        rows, down_part = group_work(inputs, grads, gate_cols, up_cols, down_rows, route, gate)
        handed, down_part = finish(rows, grads_behind, down_part)
        return handed[None], down_part[None]
    _, weight, pick = slot_picks(route, gate, live)
    pick_mat = pick.astype(jnp.bfloat16).reshape(tok_rows, live * CAP)
    rows_in = lax.dot_general(pick_mat, inputs, ROWS_FIRST, preferred_element_type=jnp.float32)
    chosen = lax.dot_general(pick_mat, grads, ROWS_FIRST, preferred_element_type=jnp.float32)
    slot_gate = jnp.sum(pick.astype(jnp.float32) * weight[:, :, None], axis=0).reshape(-1, 1)
    rows = jnp.stack([rows_in.astype(jnp.bfloat16), (chosen * slot_gate).astype(jnp.bfloat16)])
    summed, down_part = plain_work(rows, gate_cols, up_cols, down_rows)
    branch = jnp.dot(pick_mat, summed, preferred_element_type=jnp.float32)
    input_grad = (grads.astype(jnp.float32) + branch).astype(jnp.bfloat16)
    return other_core(input_grad)[None], down_part[None]


def solution(mesh):
    return jax.shard_map(
        body,
        mesh=mesh,
        in_specs=(
            P("pipe", "expert", None),
            P("pipe", "expert", None),
            P("pipe", None, "expert"),
            P("pipe", None, "expert"),
            P("pipe", "expert", None),
            P("pipe", "expert", None),
            P("pipe", "expert", None),
        ),
        out_specs=(P("pipe", "expert", None), P("pipe", "expert", None)),
        check_vma=False,
    )
```

```python
import jax
import jax.numpy as jnp
from jax import lax
from jax.experimental import pallas as pl
from jax.experimental.pallas import tpu as pltpu
from jax.sharding import PartitionSpec as P

SHARDS = 16
CAP = 5
PIECES = 8
MESH = pl.DeviceIdType.MESH
CONTRACT_LAST = (((1,), (1,)), ((), ()))
ROWS_FIRST = (((0,), (0,)), ((), ()))


def hidden_grads(gate_pre, up_pre, back_hidden):
    sigma = jax.nn.sigmoid(gate_pre)
    silu_gate = gate_pre * sigma
    hidden = silu_gate * up_pre
    grad_gate = back_hidden * up_pre * sigma * (1.0 + gate_pre * (1.0 - sigma))
    grad_up = back_hidden * silu_gate
    return hidden, grad_gate, grad_up


def flip(z, k):
    if k == 0:
        return z
    if k == 1:
        return z + 1 - 2 * lax.rem(z, 2)
    if k == 2:
        return lax.rem(z + 2, 4)
    return 3 - z


def pick_slots(route, gate):
    tok = route.shape[1]
    hit = route == 0
    member = jnp.sum(jnp.where(hit, 1.0, 0.0), axis=0, keepdims=True)
    earlier = lax.broadcasted_iota(jnp.int32, (tok, tok), 0) < lax.broadcasted_iota(
        jnp.int32, (tok, tok), 1
    )
    member8 = jnp.broadcast_to(member, (8, tok))
    position = jnp.dot(
        member8.astype(jnp.bfloat16),
        jnp.where(earlier, 1.0, 0.0).astype(jnp.bfloat16),
        preferred_element_type=jnp.float32,
    )
    slot = lax.broadcasted_iota(jnp.int32, (8, tok), 0).astype(jnp.float32)
    pick = jnp.where((member8 == 1.0) & (position == slot), 1.0, 0.0)
    weight = jnp.sum(jnp.where(hit, gate, 0.0), axis=0, keepdims=True)
    return pick, jnp.sum(pick * weight, axis=1, keepdims=True)


def swap_order(outer, inner):
    size = outer * inner
    r = lax.broadcasted_iota(jnp.int32, (size, size), 0)
    c = lax.broadcasted_iota(jnp.int32, (size, size), 1)
    source = lax.rem(r, outer) * inner + r // outer
    return jnp.where(c == source, 1.0, 0.0).astype(jnp.bfloat16)


def group_kernel(
    x_hbm, g_hbm, wg_hbm, wu_hbm, wd_hbm, route_hbm, gate_hbm,
    rows_v, base_v, down_v,
    route_v, gate_v, pick_v, x_v, g_v, wgu, wd_v, staged, plain, plain_in, gath, xf, gf, pfull, part,
    diag_in, fwd_x, fwd_y, in_x, in_y, zsum, in_z,
    load_sem, z_send, z_recv, xy_send, xy_recv, d_send, d_recv, dz_send, dz_recv,
    p_send, p_recv, t_send, t_recv, b_send, b_recv, s1_send, s1_recv, s2_send, s2_recv, s3_send, s3_recv,
):
    slots, piece = staged.shape[0], staged.shape[2]
    block = wd_v.shape[0]
    pipe = lax.axis_index("pipe")
    me = lax.axis_index("expert")
    base = (me // SHARDS) * SHARDS
    local = lax.rem(me, SHARDS)
    z = local // 4
    xy = lax.rem(local, 4)
    y, x = xy // 2, lax.rem(xy, 2)
    at_x, at_y, at_d = y * 2 + 1 - x, (1 - y) * 2 + x, 3 - xy

    def device(p, zz, spot):
        return {"pipe": p, "expert": base + zz * 4 + spot}

    x_dev, y_dev = device(pipe, z, at_x), device(pipe, z, at_y)
    z_dev = [device(pipe, flip(z, k), xy) for k in range(4)]
    back_dev = [device(1 - pipe, flip(z, k), xy) for k in range(4)]

    barrier = pltpu.get_barrier_semaphore()
    for other in [x_dev, y_dev] + z_dev[1:] + back_dev:
        pl.semaphore_signal(barrier, inc=1, device_id=other, device_id_type=MESH)

    def cols(q):
        return pl.ds(q * piece, piece)

    small = [
        pltpu.make_async_copy(route_hbm, route_v, load_sem.at[0]),
        pltpu.make_async_copy(gate_hbm, gate_v, load_sem.at[1]),
    ]
    row_loads = [
        [
            pltpu.make_async_copy(src.at[:, cols(q)], dst.at[:, cols(q)],
                                  load_sem.at[5 + kind * PIECES + q])
            for q in range(PIECES)
        ]
        for kind, (src, dst) in enumerate(((x_hbm, x_v), (g_hbm, g_v)))
    ]
    weights = [
        pltpu.make_async_copy(wg_hbm, wgu.at[:, :, pl.ds(0, block)], load_sem.at[2]),
        pltpu.make_async_copy(wu_hbm, wgu.at[:, :, pl.ds(block, block)], load_sem.at[3]),
        pltpu.make_async_copy(wd_hbm, wd_v, load_sem.at[4]),
    ]
    for copy in small + row_loads[0] + row_loads[1]:
        copy.start()
    for copy in small:
        copy.wait()
    pick, coef = pick_slots(route_v[...], gate_v[...])
    pick_v[...] = pick
    pick_mat = pick.astype(jnp.bfloat16)

    for kind in range(2):
        source = x_v if kind == 0 else g_v
        for q in range(PIECES):
            row_loads[kind][q].wait()
            rows = jnp.dot(
                pick_mat, source[:, q * piece:(q + 1) * piece], preferred_element_type=jnp.float32
            )
            scaled = rows if kind == 0 else rows * coef
            for i in range(slots):
                staged[i, kind * PIECES + q:kind * PIECES + q + 1, :] = scaled[i:i + 1, :]
                if kind == 1:
                    plain[i, q:q + 1, :] = rows[i:i + 1, :]

    def index(spot, k):
        return (k % 2) * 8 + spot * 2 + lax.rem(z // 2 + k // 2, 2)

    own = index(xy, 0)
    for i in range(slots):
        gath[own, i] = staged[i].astype(jnp.bfloat16)
    plain_in[0] = plain[...].astype(jnp.bfloat16)
    for copy in weights:
        copy.start()
    pl.semaphore_wait(barrier, 9)

    def remote(src, dst, send, recv, to):
        return pltpu.make_async_remote_copy(
            src_ref=src, dst_ref=dst, send_sem=send, recv_sem=recv, device_id=to,
            device_id_type=MESH,
        )

    sent = []

    def start(copy):
        copy.start()
        sent.append(copy)
        return copy

    for k in (2, 1, 3):
        start(remote(gath.at[own], gath.at[(k % 2) * 8 + xy * 2 + z // 2],
                     z_send.at[k], z_recv.at[k], z_dev[k]))

    def halves(k):
        if k % 2 == 1:
            return (pl.ds(0, slots),)
        cut = 3 if k == 0 else 2
        return (pl.ds(0, cut), pl.ds(cut, slots - cut))

    def slab(spot, k, half):
        return gath.at[index(spot, k), halves(k)[half]]

    def over(axis, k, half):
        ref = slab(xy, k, half)
        return remote(ref, ref, xy_send.at[axis, k, half], xy_recv.at[axis, k, half],
                      x_dev if axis == 0 else y_dev)

    def to_plane(k):
        if k % 2 == 1:
            start(over(0, k, 0))
            start(over(1, k, 0))
        else:
            start(over(0, k, 0))
            start(over(1, k, 1))
            start(over(0, k, 1))
            start(over(1, k, 0))

    def arrived(axis, k, half):
        ref = slab(at_x if axis == 0 else at_y, k, half)
        remote(ref, ref, xy_send.at[axis, k, half], xy_recv.at[axis, k, half], x_dev).wait_recv()

    def to_corner(k):
        arrived(0, k, 0)
        ref = slab(at_x, k, 0)
        start(remote(ref, ref, d_send.at[k // 2, 0], d_recv.at[k // 2, 0], y_dev))
        arrived(1, k, 1)
        ref = slab(at_y, k, 1)
        start(remote(ref, ref, d_send.at[k // 2, 1], d_recv.at[k // 2, 1], x_dev))

    def corner_arrived(k):
        for half in range(2):
            ref = slab(at_d, k, half)
            remote(ref, ref, d_send.at[k // 2, half], d_recv.at[k // 2, half], y_dev).wait_recv()

    def z_arrived(k):
        ref = gath.at[index(xy, k)]
        remote(ref, ref, z_send.at[k], z_recv.at[k], z_dev[k]).wait_recv()

    def corner_over_z(k):
        source = index(at_d, k)
        return remote(gath.at[source], gath.at[8 + source], dz_send.at[k // 2],
                      dz_recv.at[k // 2], z_dev[1])

    to_plane(0)
    plain_copy = start(remote(plain_in.at[0], plain_in.at[1], p_send, p_recv, back_dev[0]))
    width = x_v.shape[1]
    pick_copy = start(
        remote(pick_v, rows_v.at[:, pl.ds(width, pick_v.shape[1])], t_send, t_recv, back_dev[0])
    )
    base_copy = start(remote(g_v, base_v, b_send, b_recv, back_dev[0]))
    z_arrived(2)
    to_plane(2)
    to_corner(0)
    to_corner(2)
    z_arrived(1)
    to_plane(1)
    corner_arrived(0)
    start(corner_over_z(0))
    z_arrived(3)
    to_plane(3)
    corner_arrived(2)
    start(corner_over_z(2))

    group_rows = slots * 8
    to_rows = swap_order(8, 2 * PIECES)
    to_units = swap_order(PIECES, 8)
    chunks = ((0, 3), (3, slots - 3))

    def compute(r):
        for i in range(slots):
            packed = gath[r * 8:(r + 1) * 8, i].reshape(8 * 2 * PIECES, piece)
            ordered = jnp.dot(to_rows, packed, preferred_element_type=jnp.float32)
            at = r * group_rows + i * 8
            for q in range(PIECES):
                xf[q, at:at + 8, :] = ordered[q * 8:(q + 1) * 8].astype(jnp.bfloat16)
                gf[q, at:at + 8, :] = ordered[
                    (PIECES + q) * 8:(PIECES + q + 1) * 8
                ].astype(jnp.bfloat16)
        mine = slice(r * group_rows, (r + 1) * group_rows)
        pre = jnp.zeros((group_rows, 2 * block), jnp.float32)
        back = jnp.zeros((group_rows, block), jnp.float32)
        for q in range(PIECES):
            pre = pre + jnp.dot(xf[q, mine, :], wgu[q], preferred_element_type=jnp.float32)
            back = back + lax.dot_general(
                gf[q, mine, :], wd_v[:, q * piece:(q + 1) * piece], CONTRACT_LAST,
                preferred_element_type=jnp.float32,
            )
        hidden, grad_gate, grad_up = hidden_grads(pre[:, :block], pre[:, block:], back)
        grad_both = jnp.concatenate(
            [grad_gate.astype(jnp.bfloat16), grad_up.astype(jnp.bfloat16)], axis=1
        )
        return hidden, grad_both

    def diagonal(r, c, half):
        lo, count = chunks[c]
        at = pl.ds(lo, count)
        return remote(part.at[r, at, at_d, half], diag_in.at[r, at, half],
                      s1_send.at[r, c, half], s1_recv.at[r, c, half],
                      y_dev if half == 0 else x_dev)

    def direct(r, c, half):
        lo, count = chunks[c]
        at = pl.ds(lo, count)
        if half == 1:
            return remote(part.at[r, at, at_x, 1], in_x.at[r, at, 1], s1_send.at[r, c, 2],
                          s1_recv.at[r, c, 2], x_dev)
        return remote(part.at[r, at, at_y, 0], in_y.at[r, at, 0], s1_send.at[r, c, 3],
                      s1_recv.at[r, c, 3], y_dev)

    def passed(r, c, half):
        lo, count = chunks[c]
        at = pl.ds(lo, count)
        if half == 0:
            return remote(fwd_x.at[r, at], in_x.at[r, at, 0], s2_send.at[r, c, 0],
                          s2_recv.at[r, c, 0], x_dev)
        return remote(fwd_y.at[r, at], in_y.at[r, at, 1], s2_send.at[r, c, 1],
                      s2_recv.at[r, c, 1], y_dev)

    def homeward(r, c, k):
        lo, count = chunks[c]
        at = pl.ds(lo, count)
        return remote(zsum.at[r, at, lax.rem(z // 2 + k // 2, 2)], in_z.at[k, at],
                      s3_send.at[c, k], s3_recv.at[c, k], back_dev[k])

    def send_shares(r, grad_both):
        for q in range(PIECES):
            share = lax.dot_general(
                grad_both, wgu[q], CONTRACT_LAST, preferred_element_type=jnp.float32
            ).astype(jnp.bfloat16)
            for i in range(slots):
                pfull[r, i, q * 8:(q + 1) * 8, :] = share[i * 8:(i + 1) * 8]
        for c, (lo, count) in enumerate(chunks):
            for i in range(lo, lo + count):
                units = jnp.dot(to_units, pfull[r, i], preferred_element_type=jnp.float32)
                part[r, i] = units.reshape(4, 2, PIECES, piece).astype(jnp.bfloat16)
            for half in range(2):
                start(diagonal(r, c, half))
        for c in range(2):
            for half in range(2):
                start(direct(r, c, half))

    def pass_on(r):
        for c, (lo, count) in enumerate(chunks):
            for half in range(2):
                diagonal(r, c, half).wait_recv()
                spot, out = (at_x, fwd_x) if half == 0 else (at_y, fwd_y)
                for i in range(lo, lo + count):
                    out[r, i] = (
                        part[r, i, spot, half].astype(jnp.float32)
                        + diag_in[r, i, half].astype(jnp.float32)
                    ).astype(jnp.bfloat16)
                start(passed(r, c, half))

    def send_home(r):
        for c, (lo, count) in enumerate(chunks):
            for half in range(2):
                direct(r, c, half).wait_recv()
                passed(r, c, half).wait_recv()
            for i in range(lo, lo + count):
                zsum[r, i] = (
                    part[r, i, xy].astype(jnp.float32) + in_x[r, i].astype(jnp.float32)
                    + in_y[r, i].astype(jnp.float32)
                ).astype(jnp.bfloat16)
            for k in (r + 2, r):
                start(homeward(r, c, k))

    arrived(0, 0, 1)
    arrived(1, 0, 0)
    arrived(0, 2, 1)
    arrived(1, 2, 0)
    for copy in weights:
        copy.wait()
    hidden_a, grad_both = compute(0)
    send_shares(0, grad_both)
    for k in (1, 3):
        arrived(0, k, 0)
        arrived(1, k, 0)
    for k in (0, 2):
        corner_over_z(k).wait_recv()
    hidden_b, grad_both = compute(1)
    pass_on(0)
    send_shares(1, grad_both)
    hidden_t = jnp.transpose(jnp.concatenate([hidden_a, hidden_b], axis=0)).astype(jnp.bfloat16)

    def down_piece(q):
        down_v[:, q * piece:(q + 1) * piece] = jnp.dot(
            hidden_t, gf[q], preferred_element_type=jnp.float32
        ).astype(jnp.bfloat16)

    send_home(0)
    for q in range(PIECES // 2):
        down_piece(q)
    pass_on(1)
    for q in range(PIECES // 2, PIECES):
        down_piece(q)
    send_home(1)

    plain_copy.wait_recv()
    pick_copy.wait_recv()
    rows_v[slots:, :width] = jnp.zeros((rows_v.shape[0] - slots, width), jnp.float32)
    for c, (lo, count) in enumerate(chunks):
        for k in range(4):
            homeward(k % 2, c, k).wait_recv()
        for i in range(lo, lo + count):
            total = plain_in[1, i].astype(jnp.float32)
            for k in range(4):
                total = total + in_z[k, i].astype(jnp.float32)
            for q in range(PIECES):
                rows_v[i:i + 1, q * piece:(q + 1) * piece] = total[q:q + 1, :]
    base_copy.wait_recv()
    for copy in sent:
        copy.wait_send()


def group_work(inputs, grads, gate_cols, up_cols, down_rows, route, gate):
    tok, width = inputs.shape
    block = gate_cols.shape[1]
    piece = width // PIECES
    bf16 = jnp.bfloat16
    whole = pl.BlockSpec(memory_space=pl.ANY)
    near = pl.BlockSpec(memory_space=pltpu.VMEM)
    dma = pltpu.SemaphoreType.DMA
    pairs = pltpu.VMEM((2, CAP, 2, PIECES, piece), bf16)
    singles = pltpu.VMEM((2, CAP, PIECES, piece), bf16)
    return pl.pallas_call(
        group_kernel,
        out_shape=(
            pltpu.VMEM((8, width + tok), jnp.float32),
            pltpu.VMEM((tok, width), bf16),
            pltpu.VMEM((block, width), bf16),
        ),
        in_specs=[whole] * 7,
        out_specs=(near, near, near),
        scratch_shapes=[
            pltpu.VMEM(route.shape[::-1], jnp.int32),
            pltpu.VMEM(gate.shape[::-1], jnp.float32),
            pltpu.VMEM((8, tok), jnp.float32),
            pltpu.VMEM((tok, width), bf16),
            pltpu.VMEM((tok, width), bf16),
            pltpu.VMEM((PIECES, piece, 2 * block), bf16),
            pltpu.VMEM((block, width), bf16),
            pltpu.VMEM((CAP, 2 * PIECES, piece), jnp.float32),
            pltpu.VMEM((CAP, PIECES, piece), jnp.float32),
            singles,
            pltpu.VMEM((SHARDS, CAP, 2 * PIECES, piece), bf16),
            pltpu.VMEM((PIECES, CAP * SHARDS, piece), bf16),
            pltpu.VMEM((PIECES, CAP * SHARDS, piece), bf16),
            pltpu.VMEM((2, CAP, 8 * PIECES, piece), bf16),
            pltpu.VMEM((2, CAP, 4, 2, PIECES, piece), bf16),
            pairs,
            singles,
            singles,
            pairs,
            pairs,
            pairs,
            pltpu.VMEM((4, CAP, PIECES, piece), bf16),
            dma((5 + 2 * PIECES,)), dma((4,)), dma((4,)), dma((2, 4, 2)),
            dma((2, 4, 2)), dma((2, 2)), dma((2, 2)), dma((2,)), dma((2,)), dma, dma, dma, dma,
            dma, dma,
            dma((2, 2, 4)), dma((2, 2, 4)), dma((2, 2, 2)), dma((2, 2, 2)),
            dma((2, 4)), dma((2, 4)),
        ],
        compiler_params=pltpu.CompilerParams(
            collective_id=0, has_side_effects=True, vmem_limit_bytes=40 * 2**20
        ),
        cost_estimate=pl.CostEstimate(
            flops=12 * CAP * SHARDS * width * block, bytes_accessed=14 * tok * width,
            transcendentals=CAP * SHARDS * block,
        ),
        name="relay_group",
    )(*(
        pltpu.with_memory_space_constraint(operand, pltpu.HBM)
        for operand in (
            inputs, grads, gate_cols.reshape(PIECES, piece, block),
            up_cols.reshape(PIECES, piece, block), down_rows, route.T, gate.T,
        )
    ))


def finish_kernel(rows_v, base_v, down_v, handed_out, down_out, done_v, sem, down_sem):
    width = base_v.shape[1]
    piece = width // PIECES
    halves = down_v.shape[0] // 2
    downs = [
        pltpu.make_async_copy(down_v.at[pl.ds(h * halves, halves)],
                              down_out.at[pl.ds(h * halves, halves)], down_sem.at[h])
        for h in range(2)
    ]
    for copy in downs:
        copy.start()
    stores = [
        pltpu.make_async_copy(done_v.at[:, pl.ds(q * piece, piece)],
                              handed_out.at[:, pl.ds(q * piece, piece)], sem.at[q])
        for q in range(PIECES)
    ]
    named = jnp.transpose(rows_v[:, width:])
    changed = jnp.sum(named, axis=1, keepdims=True) > 0.0
    named = named.astype(jnp.bfloat16)
    for q in range(PIECES):
        at = slice(q * piece, (q + 1) * piece)
        placed = jnp.dot(
            named, rows_v[:, at].astype(jnp.bfloat16), preferred_element_type=jnp.float32
        )
        done_v[:, at] = jnp.where(changed, placed, base_v[:, at].astype(jnp.float32)).astype(
            jnp.bfloat16
        )
        stores[q].start()
    for copy in stores + downs:
        copy.wait()


def finish(rows, base, down):
    whole = pl.BlockSpec(memory_space=pl.ANY)
    near = pl.BlockSpec(memory_space=pltpu.VMEM)
    return pl.pallas_call(
        finish_kernel,
        out_shape=(
            jax.ShapeDtypeStruct(base.shape, base.dtype),
            jax.ShapeDtypeStruct(down.shape, down.dtype),
        ),
        in_specs=[near] * 3,
        out_specs=(whole, whole),
        scratch_shapes=[
            pltpu.VMEM(base.shape, base.dtype),
            pltpu.SemaphoreType.DMA((PIECES,)),
            pltpu.SemaphoreType.DMA((2,)),
        ],
        compiler_params=pltpu.CompilerParams(vmem_limit_bytes=24 * 2**20),
        cost_estimate=pl.CostEstimate(
            flops=16 * base.size, bytes_accessed=4 * base.size, transcendentals=0
        ),
        name="relay_finish",
    )(rows, base, down)


def plain_work(rows, gate_cols, up_cols, down_rows):
    width = lax.axis_size("expert")
    live = width // SHARDS
    across = [[g * SHARDS + j for g in range(live)] for j in range(SHARDS)]
    within = [[g * SHARDS + j for j in range(SHARDS)] for g in range(live)]
    kinds, count, model_width = rows.shape
    if live > 1:
        rows = lax.all_to_all(
            rows, "expert", split_axis=1, concat_axis=1, tiled=True, axis_index_groups=across
        )
    got = lax.all_gather(rows, "expert", axis=1, tiled=True, axis_index_groups=within)
    flat_in, flat_grad = got[0], got[1]
    gate_pre = jnp.dot(flat_in, gate_cols, preferred_element_type=jnp.float32)
    up_pre = jnp.dot(flat_in, up_cols, preferred_element_type=jnp.float32)
    back = lax.dot_general(flat_grad, down_rows, CONTRACT_LAST, preferred_element_type=jnp.float32)
    hidden, grad_gate, grad_up = hidden_grads(gate_pre, up_pre, back)
    share = lax.dot_general(
        grad_gate.astype(jnp.bfloat16), gate_cols, CONTRACT_LAST,
        preferred_element_type=jnp.float32,
    ) + lax.dot_general(
        grad_up.astype(jnp.bfloat16), up_cols, CONTRACT_LAST, preferred_element_type=jnp.float32
    )
    summed = lax.psum_scatter(
        share.astype(jnp.bfloat16), "expert", scatter_dimension=0, tiled=True,
        axis_index_groups=within,
    )
    if live > 1:
        summed = lax.all_to_all(
            summed, "expert", split_axis=0, concat_axis=0, tiled=True, axis_index_groups=across
        )
    down_part = lax.dot_general(
        hidden.astype(jnp.bfloat16), flat_grad, ROWS_FIRST, preferred_element_type=jnp.float32
    ).astype(jnp.bfloat16)
    return summed, down_part


def slot_picks(route, gate, live):
    hit = route[:, :, None] == jnp.arange(live, dtype=jnp.int32)
    member = jnp.sum(hit.astype(jnp.int32), axis=1)
    weight = jnp.sum(jnp.where(hit, gate[:, :, None], 0.0), axis=1)
    position = jnp.cumsum(member, axis=0) - member
    pick = (member[:, :, None] == 1) & (
        position[:, :, None] == jnp.arange(CAP, dtype=jnp.int32)
    )
    return member, weight, pick


def other_core(value):
    return lax.ppermute(value, "pipe", [(0, 1), (1, 0)])


def body(section_inputs, output_grads, w_gate, w_up, w_down, route_ids, route_gates):
    inputs, grads, route, gate = section_inputs[0], output_grads[0], route_ids[0], route_gates[0]
    gate_cols, up_cols, down_rows = w_gate[0], w_up[0], w_down[0]
    tok_rows = inputs.shape[0]
    live = lax.axis_size("expert") // SHARDS
    if live == 1:
        rows, base, down_part = group_work(
            inputs, grads, gate_cols, up_cols, down_rows, route, gate
        )
        handed, down_part = finish(rows, base, down_part)
        return handed[None], down_part[None]
    _, weight, pick = slot_picks(route, gate, live)
    pick_mat = pick.astype(jnp.bfloat16).reshape(tok_rows, live * CAP)
    rows_in = lax.dot_general(pick_mat, inputs, ROWS_FIRST, preferred_element_type=jnp.float32)
    chosen = lax.dot_general(pick_mat, grads, ROWS_FIRST, preferred_element_type=jnp.float32)
    slot_gate = jnp.sum(pick.astype(jnp.float32) * weight[:, :, None], axis=0).reshape(-1, 1)
    rows = jnp.stack([rows_in.astype(jnp.bfloat16), (chosen * slot_gate).astype(jnp.bfloat16)])
    summed, down_part = plain_work(rows, gate_cols, up_cols, down_rows)
    branch = jnp.dot(pick_mat, summed, preferred_element_type=jnp.float32)
    input_grad = (grads.astype(jnp.float32) + branch).astype(jnp.bfloat16)
    return other_core(input_grad)[None], down_part[None]


def solution(mesh):
    return jax.shard_map(
        body,
        mesh=mesh,
        in_specs=(
            P("pipe", "expert", None),
            P("pipe", "expert", None),
            P("pipe", None, "expert"),
            P("pipe", None, "expert"),
            P("pipe", "expert", None),
            P("pipe", "expert", None),
            P("pipe", "expert", None),
        ),
        out_specs=(P("pipe", "expert", None), P("pipe", "expert", None)),
        check_vma=False,
    )
```

```python
import jax
import jax.numpy as jnp
from jax import lax
from jax.experimental import pallas as pl
from jax.experimental.pallas import tpu as pltpu
from jax.sharding import PartitionSpec as P

SHARDS = 16
CAP = 5
PIECES = 8
MESH = pl.DeviceIdType.MESH
CONTRACT_LAST = (((1,), (1,)), ((), ()))
ROWS_FIRST = (((0,), (0,)), ((), ()))


def hidden_grads(gate_pre, up_pre, back_hidden):
    sigma = jax.nn.sigmoid(gate_pre)
    silu_gate = gate_pre * sigma
    hidden = silu_gate * up_pre
    grad_gate = back_hidden * up_pre * sigma * (1.0 + gate_pre * (1.0 - sigma))
    grad_up = back_hidden * silu_gate
    return hidden, grad_gate, grad_up


def flip(z, k):
    if k == 0:
        return z
    if k == 1:
        return z + 1 - 2 * lax.rem(z, 2)
    if k == 2:
        return lax.rem(z + 2, 4)
    return 3 - z


def pick_slots(route, gate):
    tok = route.shape[1]
    hit = route == 0
    member = jnp.sum(jnp.where(hit, 1.0, 0.0), axis=0, keepdims=True)
    earlier = lax.broadcasted_iota(jnp.int32, (tok, tok), 0) < lax.broadcasted_iota(
        jnp.int32, (tok, tok), 1
    )
    member8 = jnp.broadcast_to(member, (8, tok))
    position = jnp.dot(
        member8.astype(jnp.bfloat16),
        jnp.where(earlier, 1.0, 0.0).astype(jnp.bfloat16),
        preferred_element_type=jnp.float32,
    )
    slot = lax.broadcasted_iota(jnp.int32, (8, tok), 0).astype(jnp.float32)
    pick = jnp.where((member8 == 1.0) & (position == slot), 1.0, 0.0)
    weight = jnp.sum(jnp.where(hit, gate, 0.0), axis=0, keepdims=True)
    return pick, jnp.sum(pick * weight, axis=1, keepdims=True)


def swap_order(outer, inner):
    size = outer * inner
    r = lax.broadcasted_iota(jnp.int32, (size, size), 0)
    c = lax.broadcasted_iota(jnp.int32, (size, size), 1)
    source = lax.rem(r, outer) * inner + r // outer
    return jnp.where(c == source, 1.0, 0.0).astype(jnp.bfloat16)


def group_kernel(
    x_hbm, g_hbm, wg_hbm, wu_hbm, wd_hbm, route_hbm, gate_hbm,
    rows_v, base_v, down_v,
    route_v, gate_v, pick_v, x_v, g_v, wgu, wd_v, staged, plain, plain_in, gath, xf, gf, pfull, part,
    diag_in, fwd_x, fwd_y, in_x, in_y, zsum, in_z,
    load_sem, z_send, z_recv, xy_send, xy_recv, d_send, d_recv, dz_send, dz_recv,
    p_send, p_recv, t_send, t_recv, b_send, b_recv, s1_send, s1_recv, s2_send, s2_recv, s3_send, s3_recv,
):
    slots, piece = staged.shape[0], staged.shape[2]
    block = wd_v.shape[0]
    pipe = lax.axis_index("pipe")
    me = lax.axis_index("expert")
    base = (me // SHARDS) * SHARDS
    local = lax.rem(me, SHARDS)
    z = local // 4
    xy = lax.rem(local, 4)
    y, x = xy // 2, lax.rem(xy, 2)
    at_x, at_y, at_d = y * 2 + 1 - x, (1 - y) * 2 + x, 3 - xy

    def device(p, zz, spot):
        return {"pipe": p, "expert": base + zz * 4 + spot}

    x_dev, y_dev = device(pipe, z, at_x), device(pipe, z, at_y)
    z_dev = [device(pipe, flip(z, k), xy) for k in range(4)]
    back_dev = [device(1 - pipe, flip(z, k), xy) for k in range(4)]

    barrier = pltpu.get_barrier_semaphore()
    for other in [x_dev, y_dev] + z_dev[1:] + back_dev:
        pl.semaphore_signal(barrier, inc=1, device_id=other, device_id_type=MESH)

    def cols(q):
        return pl.ds(q * piece, piece)

    small = [
        pltpu.make_async_copy(route_hbm, route_v, load_sem.at[0]),
        pltpu.make_async_copy(gate_hbm, gate_v, load_sem.at[1]),
    ]
    row_loads = [
        [
            pltpu.make_async_copy(src.at[:, cols(q)], dst.at[:, cols(q)],
                                  load_sem.at[5 + kind * PIECES + q])
            for q in range(PIECES)
        ]
        for kind, (src, dst) in enumerate(((x_hbm, x_v), (g_hbm, g_v)))
    ]
    weights = [
        pltpu.make_async_copy(wg_hbm, wgu.at[:, pl.ds(0, block)], load_sem.at[2]),
        pltpu.make_async_copy(wu_hbm, wgu.at[:, pl.ds(block, block)], load_sem.at[3]),
        pltpu.make_async_copy(wd_hbm, wd_v, load_sem.at[4]),
    ]
    for copy in small + row_loads[0] + row_loads[1]:
        copy.start()
    for copy in small:
        copy.wait()
    pick, coef = pick_slots(route_v[...], gate_v[...])
    pick_v[...] = pick
    pick_mat = pick.astype(jnp.bfloat16)

    def index(spot, k):
        return (k % 2) * 8 + spot * 2 + lax.rem(z // 2 + k // 2, 2)

    own = index(xy, 0)

    def remote(src, dst, send, recv, to):
        return pltpu.make_async_remote_copy(
            src_ref=src, dst_ref=dst, send_sem=send, recv_sem=recv, device_id=to,
            device_id_type=MESH,
        )

    sent = []

    def start(copy):
        copy.start()
        sent.append(copy)
        return copy

    def slab(spot, k, kind):
        return gath.at[kind, index(spot, k)]

    def over_z(kind):
        for k in (2, 1, 3):
            start(remote(slab(xy, 0, kind), gath.at[kind, (k % 2) * 8 + xy * 2 + z // 2],
                         z_send.at[k, kind], z_recv.at[k, kind], z_dev[k]))

    def to_plane(k, kind):
        ref = slab(xy, k, kind)
        for axis, to in ((kind, (x_dev, y_dev)[kind]), (1 - kind, (y_dev, x_dev)[kind])):
            start(remote(ref, ref, xy_send.at[axis, k, kind], xy_recv.at[axis, k, kind], to))

    def arrived(axis, k, kind):
        ref = slab(at_x if axis == 0 else at_y, k, kind)
        remote(ref, ref, xy_send.at[axis, k, kind], xy_recv.at[axis, k, kind], x_dev).wait_recv()

    def to_corner(k):
        for kind, (spot, to) in enumerate(((at_x, y_dev), (at_y, x_dev))):
            arrived(kind, k, kind)
            ref = slab(spot, k, kind)
            start(remote(ref, ref, d_send.at[k // 2, kind], d_recv.at[k // 2, kind], to))

    def z_arrived(k, kind):
        ref = slab(xy, k, kind)
        remote(ref, ref, z_send.at[k, kind], z_recv.at[k, kind], z_dev[k]).wait_recv()

    def corner_over_z(k, kind):
        source = index(at_d, k)
        return remote(gath.at[kind, source], gath.at[kind, 8 + source], dz_send.at[k // 2, kind],
                      dz_recv.at[k // 2, kind], z_dev[1])

    def corner_passed(k):
        for kind in range(2):
            ref = slab(at_d, k, kind)
            remote(ref, ref, d_send.at[k // 2, kind], d_recv.at[k // 2, kind], y_dev).wait_recv()
            start(corner_over_z(k, kind))

    tiles = piece // 128
    for kind in range(2):
        source = x_v if kind == 0 else g_v
        for q in range(PIECES):
            row_loads[kind][q].wait()
            rows = jnp.dot(
                pick_mat, source[:, q * piece:(q + 1) * piece], preferred_element_type=jnp.float32
            )
            scaled = rows if kind == 0 else rows * coef
            for i in range(slots):
                staged[i, q:q + 1, :] = scaled[i:i + 1, :]
                if kind == 1:
                    for m in range(tiles):
                        j, sub = divmod(q * tiles + m, PIECES)
                        plain[i, sub:sub + 1, j * 128:(j + 1) * 128] = rows[
                            i:i + 1, m * 128:(m + 1) * 128
                        ]
        for i in range(slots):
            gath[kind, own, i] = staged[i].astype(jnp.bfloat16)
        if kind == 0:
            pl.semaphore_wait(barrier, 9)
        over_z(kind)
        to_plane(0, kind)
    plain_in[0] = plain[...].astype(jnp.bfloat16)
    for copy in weights:
        copy.start()
    plain_copy = start(remote(plain_in.at[0], plain_in.at[1], p_send, p_recv, back_dev[0]))
    width = x_v.shape[1]
    pick_copy = start(
        remote(pick_v, rows_v.at[:, pl.ds(width, pick_v.shape[1])], t_send, t_recv, back_dev[0])
    )
    base_copy = start(remote(g_v, base_v, b_send, b_recv, back_dev[0]))
    for kind in range(2):
        z_arrived(2, kind)
        to_plane(2, kind)
    to_corner(0)
    to_corner(2)
    for kind in range(2):
        z_arrived(1, kind)
        to_plane(1, kind)
    corner_passed(0)
    for kind in range(2):
        z_arrived(3, kind)
        to_plane(3, kind)
    corner_passed(2)

    group_rows = slots * 8
    to_rows = swap_order(8, PIECES)
    to_units = swap_order(PIECES, 8)
    chunks = ((0, (tiles + 1) // 2), ((tiles + 1) // 2, tiles // 2))

    def compute(r):
        for i in range(slots):
            at = r * group_rows + i * 8
            for kind, out in enumerate((xf, gf)):
                packed = gath[kind, r * 8:(r + 1) * 8, i].astype(jnp.float32)
                ordered = jnp.dot(
                    to_rows, packed.reshape(8 * PIECES, piece).astype(jnp.bfloat16),
                    preferred_element_type=jnp.float32,
                )
                for q in range(PIECES):
                    out[q, at:at + 8, :] = ordered[q * 8:(q + 1) * 8].astype(jnp.bfloat16)
        mine = slice(r * group_rows, (r + 1) * group_rows)
        pre = jnp.zeros((group_rows, 2 * block), jnp.float32)
        back = jnp.zeros((group_rows, block), jnp.float32)
        for q in range(PIECES):
            pre = pre + jnp.dot(
                xf[q, mine, :], wgu[q * piece:(q + 1) * piece, :], preferred_element_type=jnp.float32
            )
            back = back + lax.dot_general(
                gf[q, mine, :], wd_v[:, q * piece:(q + 1) * piece], CONTRACT_LAST,
                preferred_element_type=jnp.float32,
            )
        hidden, grad_gate, grad_up = hidden_grads(pre[:, :block], pre[:, block:], back)
        grad_both = jnp.concatenate(
            [grad_gate.astype(jnp.bfloat16), grad_up.astype(jnp.bfloat16)], axis=1
        )
        return hidden, grad_both

    def diagonal(r, c, half):
        lo, count = chunks[c]
        at = pl.ds(lo * 128, count * 128)
        return remote(part.at[r, :, at_d, half, :, at], diag_in.at[r, :, half, :, at],
                      s1_send.at[r, c, half], s1_recv.at[r, c, half],
                      y_dev if half == 0 else x_dev)

    def direct(r, c, half):
        lo, count = chunks[c]
        at = pl.ds(lo * 128, count * 128)
        if half == 1:
            return remote(part.at[r, :, at_x, 1, :, at], in_x.at[r, :, 1, :, at], s1_send.at[r, c, 2],
                          s1_recv.at[r, c, 2], x_dev)
        return remote(part.at[r, :, at_y, 0, :, at], in_y.at[r, :, 0, :, at], s1_send.at[r, c, 3],
                      s1_recv.at[r, c, 3], y_dev)

    def passed(r, c, half):
        lo, count = chunks[c]
        at = pl.ds(lo * 128, count * 128)
        if half == 0:
            return remote(fwd_x.at[r, :, :, at], in_x.at[r, :, 0, :, at], s2_send.at[r, c, 0],
                          s2_recv.at[r, c, 0], x_dev)
        return remote(fwd_y.at[r, :, :, at], in_y.at[r, :, 1, :, at], s2_send.at[r, c, 1],
                      s2_recv.at[r, c, 1], y_dev)

    def homeward(r, c, k):
        lo, count = chunks[c]
        at = pl.ds(lo * 128, count * 128)
        return remote(zsum.at[r, :, lax.rem(z // 2 + k // 2, 2), :, at], in_z.at[k, :, :, at],
                      s3_send.at[c, k], s3_recv.at[c, k], back_dev[k])

    def send_shares(r, grad_both):
        for c, (lo, count) in enumerate(chunks):
            lanes = slice(lo * 128, (lo + count) * 128)
            for j in range(lo, lo + count):
                wide = PIECES * 128
                share = lax.dot_general(
                    grad_both, wgu[j * wide:(j + 1) * wide, :], CONTRACT_LAST,
                    preferred_element_type=jnp.float32,
                ).astype(jnp.bfloat16)
                for i in range(slots):
                    for q in range(PIECES):
                        pfull[r, i, q * 8:(q + 1) * 8, j * 128:(j + 1) * 128] = share[
                            i * 8:(i + 1) * 8, q * 128:(q + 1) * 128
                        ]
            for i in range(slots):
                units = jnp.dot(
                    to_units, pfull[r, i, :, lanes], preferred_element_type=jnp.float32
                )
                part[r, i, :, :, :, lanes] = units.reshape(
                    4, 2, PIECES, count * 128
                ).astype(jnp.bfloat16)
            for half in range(2):
                start(diagonal(r, c, half))
            for half in range(2):
                start(direct(r, c, half))

    def pass_on(r):
        for c, (lo, count) in enumerate(chunks):
            lanes = slice(lo * 128, (lo + count) * 128)
            for half in range(2):
                diagonal(r, c, half).wait_recv()
                spot, out = (at_x, fwd_x) if half == 0 else (at_y, fwd_y)
                for i in range(slots):
                    out[r, i, :, lanes] = (
                        part[r, i, spot, half, :, lanes].astype(jnp.float32)
                        + diag_in[r, i, half, :, lanes].astype(jnp.float32)
                    ).astype(jnp.bfloat16)
                start(passed(r, c, half))

    def send_home(r):
        for c, (lo, count) in enumerate(chunks):
            lanes = slice(lo * 128, (lo + count) * 128)
            for half in range(2):
                direct(r, c, half).wait_recv()
                passed(r, c, half).wait_recv()
            for i in range(slots):
                zsum[r, i, :, :, lanes] = (
                    part[r, i, xy, :, :, lanes].astype(jnp.float32)
                    + in_x[r, i, :, :, lanes].astype(jnp.float32)
                    + in_y[r, i, :, :, lanes].astype(jnp.float32)
                ).astype(jnp.bfloat16)
            for k in (r + 2, r):
                start(homeward(r, c, k))

    arrived(0, 0, 1)
    arrived(1, 0, 0)
    arrived(0, 2, 1)
    arrived(1, 2, 0)
    for copy in weights:
        copy.wait()
    hidden_a, grad_both = compute(0)
    send_shares(0, grad_both)
    for k in (1, 3):
        for kind in range(2):
            arrived(0, k, kind)
            arrived(1, k, kind)
    for k in (0, 2):
        for kind in range(2):
            corner_over_z(k, kind).wait_recv()
    hidden_b, grad_both = compute(1)
    pass_on(0)
    send_shares(1, grad_both)
    hidden_t = jnp.transpose(jnp.concatenate([hidden_a, hidden_b], axis=0)).astype(jnp.bfloat16)

    def down_piece(q):
        down_v[:, q * piece:(q + 1) * piece] = jnp.dot(
            hidden_t, gf[q], preferred_element_type=jnp.float32
        ).astype(jnp.bfloat16)

    send_home(0)
    for q in range(PIECES // 2):
        down_piece(q)
    pass_on(1)
    for q in range(PIECES // 2, PIECES):
        down_piece(q)
    send_home(1)

    plain_copy.wait_recv()
    pick_copy.wait_recv()
    rows_v[slots:, :width] = jnp.zeros((rows_v.shape[0] - slots, width), jnp.float32)
    for c, (lo, count) in enumerate(chunks):
        for k in range(4):
            homeward(k % 2, c, k).wait_recv()
        lanes = slice(lo * 128, (lo + count) * 128)
        for i in range(slots):
            total = plain_in[1, i, :, lanes].astype(jnp.float32)
            for k in range(4):
                total = total + in_z[k, i, :, lanes].astype(jnp.float32)
            for j in range(count):
                for q in range(PIECES):
                    at = ((lo + j) * PIECES + q) * 128
                    rows_v[i:i + 1, at:at + 128] = total[q:q + 1, j * 128:(j + 1) * 128]
    base_copy.wait_recv()
    for copy in sent:
        copy.wait_send()


def group_work(inputs, grads, gate_cols, up_cols, down_rows, route, gate):
    tok, width = inputs.shape
    block = gate_cols.shape[1]
    piece = width // PIECES
    bf16 = jnp.bfloat16
    whole = pl.BlockSpec(memory_space=pl.ANY)
    near = pl.BlockSpec(memory_space=pltpu.VMEM)
    dma = pltpu.SemaphoreType.DMA
    pairs = pltpu.VMEM((2, CAP, 2, PIECES, piece), bf16)
    singles = pltpu.VMEM((2, CAP, PIECES, piece), bf16)
    return pl.pallas_call(
        group_kernel,
        out_shape=(
            pltpu.VMEM((8, width + tok), jnp.float32),
            pltpu.VMEM((tok, width), bf16),
            pltpu.VMEM((block, width), bf16),
        ),
        in_specs=[whole] * 7,
        out_specs=(near, near, near),
        scratch_shapes=[
            pltpu.VMEM(route.shape[::-1], jnp.int32),
            pltpu.VMEM(gate.shape[::-1], jnp.float32),
            pltpu.VMEM((8, tok), jnp.float32),
            pltpu.VMEM((tok, width), bf16),
            pltpu.VMEM((tok, width), bf16),
            pltpu.VMEM((width, 2 * block), bf16),
            pltpu.VMEM((block, width), bf16),
            pltpu.VMEM((CAP, PIECES, piece), jnp.float32),
            pltpu.VMEM((CAP, PIECES, piece), jnp.float32),
            singles,
            pltpu.VMEM((2, SHARDS, CAP, PIECES, piece), bf16),
            pltpu.VMEM((PIECES, CAP * SHARDS, piece), bf16),
            pltpu.VMEM((PIECES, CAP * SHARDS, piece), bf16),
            pltpu.VMEM((2, CAP, 8 * PIECES, piece), bf16),
            pltpu.VMEM((2, CAP, 4, 2, PIECES, piece), bf16),
            pairs,
            singles,
            singles,
            pairs,
            pairs,
            pairs,
            pltpu.VMEM((4, CAP, PIECES, piece), bf16),
            dma((5 + 2 * PIECES,)), dma((4, 2)), dma((4, 2)), dma((2, 4, 2)),
            dma((2, 4, 2)), dma((2, 2)), dma((2, 2)), dma((2, 2)), dma((2, 2)), dma, dma, dma, dma,
            dma, dma,
            dma((2, 2, 4)), dma((2, 2, 4)), dma((2, 2, 2)), dma((2, 2, 2)),
            dma((2, 4)), dma((2, 4)),
        ],
        compiler_params=pltpu.CompilerParams(
            collective_id=0, has_side_effects=True, vmem_limit_bytes=40 * 2**20
        ),
        cost_estimate=pl.CostEstimate(
            flops=12 * CAP * SHARDS * width * block, bytes_accessed=14 * tok * width,
            transcendentals=CAP * SHARDS * block,
        ),
        name="relay_group",
    )(*(
        pltpu.with_memory_space_constraint(operand, pltpu.HBM)
        for operand in (
            inputs, grads, gate_cols, up_cols, down_rows, route.T, gate.T,
        )
    ))


def finish_kernel(rows_v, base_v, down_v, handed_out, down_out, done_v, sem, down_sem):
    width = base_v.shape[1]
    piece = width // PIECES
    halves = down_v.shape[0] // 2
    downs = [
        pltpu.make_async_copy(down_v.at[pl.ds(h * halves, halves)],
                              down_out.at[pl.ds(h * halves, halves)], down_sem.at[h])
        for h in range(2)
    ]
    for copy in downs:
        copy.start()
    stores = [
        pltpu.make_async_copy(done_v.at[:, pl.ds(q * piece, piece)],
                              handed_out.at[:, pl.ds(q * piece, piece)], sem.at[q])
        for q in range(PIECES)
    ]
    named = jnp.transpose(rows_v[:, width:])
    changed = jnp.sum(named, axis=1, keepdims=True) > 0.0
    named = named.astype(jnp.bfloat16)
    for q in range(PIECES):
        at = slice(q * piece, (q + 1) * piece)
        placed = jnp.dot(
            named, rows_v[:, at].astype(jnp.bfloat16), preferred_element_type=jnp.float32
        )
        done_v[:, at] = jnp.where(changed, placed, base_v[:, at].astype(jnp.float32)).astype(
            jnp.bfloat16
        )
        stores[q].start()
    for copy in stores + downs:
        copy.wait()


def finish(rows, base, down):
    whole = pl.BlockSpec(memory_space=pl.ANY)
    near = pl.BlockSpec(memory_space=pltpu.VMEM)
    return pl.pallas_call(
        finish_kernel,
        out_shape=(
            jax.ShapeDtypeStruct(base.shape, base.dtype),
            jax.ShapeDtypeStruct(down.shape, down.dtype),
        ),
        in_specs=[near] * 3,
        out_specs=(whole, whole),
        scratch_shapes=[
            pltpu.VMEM(base.shape, base.dtype),
            pltpu.SemaphoreType.DMA((PIECES,)),
            pltpu.SemaphoreType.DMA((2,)),
        ],
        compiler_params=pltpu.CompilerParams(vmem_limit_bytes=24 * 2**20),
        cost_estimate=pl.CostEstimate(
            flops=16 * base.size, bytes_accessed=4 * base.size, transcendentals=0
        ),
        name="relay_finish",
    )(rows, base, down)


def plain_work(rows, gate_cols, up_cols, down_rows):
    width = lax.axis_size("expert")
    live = width // SHARDS
    across = [[g * SHARDS + j for g in range(live)] for j in range(SHARDS)]
    within = [[g * SHARDS + j for j in range(SHARDS)] for g in range(live)]
    kinds, count, model_width = rows.shape
    if live > 1:
        rows = lax.all_to_all(
            rows, "expert", split_axis=1, concat_axis=1, tiled=True, axis_index_groups=across
        )
    got = lax.all_gather(rows, "expert", axis=1, tiled=True, axis_index_groups=within)
    flat_in, flat_grad = got[0], got[1]
    gate_pre = jnp.dot(flat_in, gate_cols, preferred_element_type=jnp.float32)
    up_pre = jnp.dot(flat_in, up_cols, preferred_element_type=jnp.float32)
    back = lax.dot_general(flat_grad, down_rows, CONTRACT_LAST, preferred_element_type=jnp.float32)
    hidden, grad_gate, grad_up = hidden_grads(gate_pre, up_pre, back)
    share = lax.dot_general(
        grad_gate.astype(jnp.bfloat16), gate_cols, CONTRACT_LAST,
        preferred_element_type=jnp.float32,
    ) + lax.dot_general(
        grad_up.astype(jnp.bfloat16), up_cols, CONTRACT_LAST, preferred_element_type=jnp.float32
    )
    summed = lax.psum_scatter(
        share.astype(jnp.bfloat16), "expert", scatter_dimension=0, tiled=True,
        axis_index_groups=within,
    )
    if live > 1:
        summed = lax.all_to_all(
            summed, "expert", split_axis=0, concat_axis=0, tiled=True, axis_index_groups=across
        )
    down_part = lax.dot_general(
        hidden.astype(jnp.bfloat16), flat_grad, ROWS_FIRST, preferred_element_type=jnp.float32
    ).astype(jnp.bfloat16)
    return summed, down_part


def slot_picks(route, gate, live):
    hit = route[:, :, None] == jnp.arange(live, dtype=jnp.int32)
    member = jnp.sum(hit.astype(jnp.int32), axis=1)
    weight = jnp.sum(jnp.where(hit, gate[:, :, None], 0.0), axis=1)
    position = jnp.cumsum(member, axis=0) - member
    pick = (member[:, :, None] == 1) & (
        position[:, :, None] == jnp.arange(CAP, dtype=jnp.int32)
    )
    return member, weight, pick


def other_core(value):
    return lax.ppermute(value, "pipe", [(0, 1), (1, 0)])


def body(section_inputs, output_grads, w_gate, w_up, w_down, route_ids, route_gates):
    inputs, grads, route, gate = section_inputs[0], output_grads[0], route_ids[0], route_gates[0]
    gate_cols, up_cols, down_rows = w_gate[0], w_up[0], w_down[0]
    tok_rows = inputs.shape[0]
    live = lax.axis_size("expert") // SHARDS
    if live == 1:
        rows, base, down_part = group_work(
            inputs, grads, gate_cols, up_cols, down_rows, route, gate
        )
        handed, down_part = finish(rows, base, down_part)
        return handed[None], down_part[None]
    _, weight, pick = slot_picks(route, gate, live)
    pick_mat = pick.astype(jnp.bfloat16).reshape(tok_rows, live * CAP)
    rows_in = lax.dot_general(pick_mat, inputs, ROWS_FIRST, preferred_element_type=jnp.float32)
    chosen = lax.dot_general(pick_mat, grads, ROWS_FIRST, preferred_element_type=jnp.float32)
    slot_gate = jnp.sum(pick.astype(jnp.float32) * weight[:, :, None], axis=0).reshape(-1, 1)
    rows = jnp.stack([rows_in.astype(jnp.bfloat16), (chosen * slot_gate).astype(jnp.bfloat16)])
    summed, down_part = plain_work(rows, gate_cols, up_cols, down_rows)
    branch = jnp.dot(pick_mat, summed, preferred_element_type=jnp.float32)
    input_grad = (grads.astype(jnp.float32) + branch).astype(jnp.bfloat16)
    return other_core(input_grad)[None], down_part[None]


def solution(mesh):
    return jax.shard_map(
        body,
        mesh=mesh,
        in_specs=(
            P("pipe", "expert", None),
            P("pipe", "expert", None),
            P("pipe", None, "expert"),
            P("pipe", None, "expert"),
            P("pipe", "expert", None),
            P("pipe", "expert", None),
            P("pipe", "expert", None),
        ),
        out_specs=(P("pipe", "expert", None), P("pipe", "expert", None)),
        check_vma=False,
    )
```

```python
import jax
import jax.numpy as jnp
from jax import lax
from jax.experimental import pallas as pl
from jax.experimental.pallas import tpu as pltpu
from jax.sharding import PartitionSpec as P

SHARDS = 16
CAP = 5
PIECES = 8
MESH = pl.DeviceIdType.MESH
CONTRACT_LAST = (((1,), (1,)), ((), ()))
ROWS_FIRST = (((0,), (0,)), ((), ()))


def hidden_grads(gate_pre, up_pre, back_hidden):
    sigma = jax.nn.sigmoid(gate_pre)
    silu_gate = gate_pre * sigma
    hidden = silu_gate * up_pre
    grad_gate = back_hidden * up_pre * sigma * (1.0 + gate_pre * (1.0 - sigma))
    grad_up = back_hidden * silu_gate
    return hidden, grad_gate, grad_up


def flip(z, k):
    if k == 0:
        return z
    if k == 1:
        return z + 1 - 2 * lax.rem(z, 2)
    if k == 2:
        return lax.rem(z + 2, 4)
    return 3 - z


def pick_slots(route, gate):
    tok = route.shape[1]
    hit = route == 0
    member = jnp.sum(jnp.where(hit, 1.0, 0.0), axis=0, keepdims=True)
    earlier = lax.broadcasted_iota(jnp.int32, (tok, tok), 0) < lax.broadcasted_iota(
        jnp.int32, (tok, tok), 1
    )
    member8 = jnp.broadcast_to(member, (8, tok))
    position = jnp.dot(
        member8.astype(jnp.bfloat16),
        jnp.where(earlier, 1.0, 0.0).astype(jnp.bfloat16),
        preferred_element_type=jnp.float32,
    )
    slot = lax.broadcasted_iota(jnp.int32, (8, tok), 0).astype(jnp.float32)
    pick = jnp.where((member8 == 1.0) & (position == slot), 1.0, 0.0)
    weight = jnp.sum(jnp.where(hit, gate, 0.0), axis=0, keepdims=True)
    return pick, jnp.sum(pick * weight, axis=1, keepdims=True)


def swap_order(outer, inner):
    size = outer * inner
    r = lax.broadcasted_iota(jnp.int32, (size, size), 0)
    c = lax.broadcasted_iota(jnp.int32, (size, size), 1)
    source = lax.rem(r, outer) * inner + r // outer
    return jnp.where(c == source, 1.0, 0.0).astype(jnp.bfloat16)


def group_kernel(
    x_hbm, g_hbm, wg_hbm, wu_hbm, wd_hbm, route_hbm, gate_hbm,
    rows_v, base_v, down_v,
    route_v, gate_v, pick_v, x_v, g_v, wgu, wd_v, staged, plain, plain_in, gath, xf, gf, pfull, part,
    diag_in, fwd_x, fwd_y, in_x, in_y, zsum, in_z,
    load_sem, z_send, z_recv, xy_send, xy_recv, d_send, d_recv, dz_send, dz_recv,
    p_send, p_recv, t_send, t_recv, b_send, b_recv, s1_send, s1_recv, s2_send, s2_recv, s3_send, s3_recv,
):
    slots, piece = staged.shape[0], staged.shape[2]
    block = wd_v.shape[0]
    pipe = lax.axis_index("pipe")
    me = lax.axis_index("expert")
    base = (me // SHARDS) * SHARDS
    local = lax.rem(me, SHARDS)
    z = local // 4
    xy = lax.rem(local, 4)
    y, x = xy // 2, lax.rem(xy, 2)
    at_x, at_y, at_d = y * 2 + 1 - x, (1 - y) * 2 + x, 3 - xy

    def device(p, zz, spot):
        return {"pipe": p, "expert": base + zz * 4 + spot}

    x_dev, y_dev = device(pipe, z, at_x), device(pipe, z, at_y)
    z_dev = [device(pipe, flip(z, k), xy) for k in range(4)]
    back_dev = [device(1 - pipe, flip(z, k), xy) for k in range(4)]

    barrier = pltpu.get_barrier_semaphore()
    for other in [x_dev, y_dev] + z_dev[1:] + back_dev:
        pl.semaphore_signal(barrier, inc=1, device_id=other, device_id_type=MESH)

    def cols(q):
        return pl.ds(q * piece, piece)

    small = [
        pltpu.make_async_copy(route_hbm, route_v, load_sem.at[0]),
        pltpu.make_async_copy(gate_hbm, gate_v, load_sem.at[1]),
    ]
    row_loads = [
        [
            pltpu.make_async_copy(src.at[:, cols(q)], dst.at[:, cols(q)],
                                  load_sem.at[5 + kind * PIECES + q])
            for q in range(PIECES)
        ]
        for kind, (src, dst) in enumerate(((x_hbm, x_v), (g_hbm, g_v)))
    ]
    weights = [
        pltpu.make_async_copy(wg_hbm, wgu.at[:, pl.ds(0, block)], load_sem.at[2]),
        pltpu.make_async_copy(wu_hbm, wgu.at[:, pl.ds(block, block)], load_sem.at[3]),
        pltpu.make_async_copy(wd_hbm, wd_v, load_sem.at[4]),
    ]
    for copy in small + row_loads[0] + row_loads[1]:
        copy.start()
    for copy in small:
        copy.wait()
    pick, coef = pick_slots(route_v[...], gate_v[...])
    pick_v[...] = pick
    pick_mat = pick.astype(jnp.bfloat16)

    def index(spot, k):
        return (k % 2) * 8 + spot * 2 + lax.rem(z // 2 + k // 2, 2)

    own = index(xy, 0)

    def remote(src, dst, send, recv, to):
        return pltpu.make_async_remote_copy(
            src_ref=src, dst_ref=dst, send_sem=send, recv_sem=recv, device_id=to,
            device_id_type=MESH,
        )

    sent = []

    def start(copy):
        copy.start()
        sent.append(copy)
        return copy

    def slab(spot, k, kind):
        return gath.at[kind, index(spot, k)]

    def over_z(kind):
        for k in (2, 1, 3):
            start(remote(slab(xy, 0, kind), gath.at[kind, (k % 2) * 8 + xy * 2 + z // 2],
                         z_send.at[k, kind], z_recv.at[k, kind], z_dev[k]))

    def to_plane(k, kind):
        ref = slab(xy, k, kind)
        for axis, to in ((kind, (x_dev, y_dev)[kind]), (1 - kind, (y_dev, x_dev)[kind])):
            start(remote(ref, ref, xy_send.at[axis, k, kind], xy_recv.at[axis, k, kind], to))

    def arrived(axis, k, kind):
        ref = slab(at_x if axis == 0 else at_y, k, kind)
        remote(ref, ref, xy_send.at[axis, k, kind], xy_recv.at[axis, k, kind], x_dev).wait_recv()

    def to_corner(k):
        for kind, (spot, to) in enumerate(((at_x, y_dev), (at_y, x_dev))):
            arrived(kind, k, kind)
            ref = slab(spot, k, kind)
            start(remote(ref, ref, d_send.at[k // 2, kind], d_recv.at[k // 2, kind], to))

    def z_arrived(k, kind):
        ref = slab(xy, k, kind)
        remote(ref, ref, z_send.at[k, kind], z_recv.at[k, kind], z_dev[k]).wait_recv()

    def corner_over_z(k, kind):
        source = index(at_d, k)
        return remote(gath.at[kind, source], gath.at[kind, 8 + source], dz_send.at[k // 2, kind],
                      dz_recv.at[k // 2, kind], z_dev[1])

    def corner_passed(k):
        for kind in range(2):
            ref = slab(at_d, k, kind)
            remote(ref, ref, d_send.at[k // 2, kind], d_recv.at[k // 2, kind], y_dev).wait_recv()
            start(corner_over_z(k, kind))

    for kind in range(2):
        source = x_v if kind == 0 else g_v
        for q in range(PIECES):
            row_loads[kind][q].wait()
            rows = jnp.dot(
                pick_mat, source[:, q * piece:(q + 1) * piece], preferred_element_type=jnp.float32
            )
            scaled = rows if kind == 0 else rows * coef
            for i in range(slots):
                staged[i, q:q + 1, :] = scaled[i:i + 1, :]
                if kind == 1:
                    plain[i, q:q + 1, :] = rows[i:i + 1, :]
        for i in range(slots):
            gath[kind, own, i] = staged[i].astype(jnp.bfloat16)
        if kind == 0:
            pl.semaphore_wait(barrier, 9)
        over_z(kind)
        to_plane(0, kind)
    plain_in[0] = plain[...].astype(jnp.bfloat16)
    for copy in weights:
        copy.start()
    plain_copy = start(remote(plain_in.at[0], plain_in.at[1], p_send, p_recv, back_dev[0]))
    width = x_v.shape[1]
    pick_copy = start(
        remote(pick_v, rows_v.at[:, pl.ds(width, pick_v.shape[1])], t_send, t_recv, back_dev[0])
    )
    base_copy = start(remote(g_v, base_v, b_send, b_recv, back_dev[0]))
    for kind in range(2):
        z_arrived(2, kind)
        to_plane(2, kind)
    to_corner(0)
    to_corner(2)
    for kind in range(2):
        z_arrived(1, kind)
        to_plane(1, kind)
    corner_passed(0)
    for kind in range(2):
        z_arrived(3, kind)
        to_plane(3, kind)
    corner_passed(2)

    group_rows = slots * 8
    to_rows = swap_order(8, PIECES)
    to_units = swap_order(PIECES, 8)
    chunks = ((0, 3), (3, slots - 3))

    def compute(r):
        for i in range(slots):
            at = r * group_rows + i * 8
            for kind, out in enumerate((xf, gf)):
                packed = gath[kind, r * 8:(r + 1) * 8, i].astype(jnp.float32)
                ordered = jnp.dot(
                    to_rows, packed.reshape(8 * PIECES, piece).astype(jnp.bfloat16),
                    preferred_element_type=jnp.float32,
                )
                for q in range(PIECES):
                    out[q, at:at + 8, :] = ordered[q * 8:(q + 1) * 8].astype(jnp.bfloat16)
        mine = slice(r * group_rows, (r + 1) * group_rows)
        pre = jnp.zeros((group_rows, 2 * block), jnp.float32)
        back = jnp.zeros((group_rows, block), jnp.float32)
        for q in range(PIECES):
            pre = pre + jnp.dot(
                xf[q, mine, :], wgu[q * piece:(q + 1) * piece, :], preferred_element_type=jnp.float32
            )
            back = back + lax.dot_general(
                gf[q, mine, :], wd_v[:, q * piece:(q + 1) * piece], CONTRACT_LAST,
                preferred_element_type=jnp.float32,
            )
        hidden, grad_gate, grad_up = hidden_grads(pre[:, :block], pre[:, block:], back)
        grad_both = jnp.concatenate(
            [grad_gate.astype(jnp.bfloat16), grad_up.astype(jnp.bfloat16)], axis=1
        )
        return hidden, grad_both

    def diagonal(r, c, half):
        lo, count = chunks[c]
        at = pl.ds(lo, count)
        return remote(part.at[r, at, at_d, half], diag_in.at[r, at, half],
                      s1_send.at[r, c, half], s1_recv.at[r, c, half],
                      y_dev if half == 0 else x_dev)

    def direct(r, c, half):
        lo, count = chunks[c]
        at = pl.ds(lo, count)
        if half == 1:
            return remote(part.at[r, at, at_x, 1], in_x.at[r, at, 1], s1_send.at[r, c, 2],
                          s1_recv.at[r, c, 2], x_dev)
        return remote(part.at[r, at, at_y, 0], in_y.at[r, at, 0], s1_send.at[r, c, 3],
                      s1_recv.at[r, c, 3], y_dev)

    def passed(r, c, half):
        lo, count = chunks[c]
        at = pl.ds(lo, count)
        if half == 0:
            return remote(fwd_x.at[r, at], in_x.at[r, at, 0], s2_send.at[r, c, 0],
                          s2_recv.at[r, c, 0], x_dev)
        return remote(fwd_y.at[r, at], in_y.at[r, at, 1], s2_send.at[r, c, 1],
                      s2_recv.at[r, c, 1], y_dev)

    def homeward(r, c, k):
        lo, count = chunks[c]
        at = pl.ds(lo, count)
        return remote(zsum.at[r, at, lax.rem(z // 2 + k // 2, 2)], in_z.at[k, at],
                      s3_send.at[c, k], s3_recv.at[c, k], back_dev[k])

    def send_shares(r, grad_both):
        for q in range(PIECES):
            share = lax.dot_general(
                grad_both, wgu[q * piece:(q + 1) * piece, :], CONTRACT_LAST, preferred_element_type=jnp.float32
            ).astype(jnp.bfloat16)
            for i in range(slots):
                pfull[r, i, q * 8:(q + 1) * 8, :] = share[i * 8:(i + 1) * 8]
        for c, (lo, count) in enumerate(chunks):
            for i in range(lo, lo + count):
                units = jnp.dot(to_units, pfull[r, i], preferred_element_type=jnp.float32)
                part[r, i] = units.reshape(4, 2, PIECES, piece).astype(jnp.bfloat16)
            for half in range(2):
                start(diagonal(r, c, half))
        for c in range(2):
            for half in range(2):
                start(direct(r, c, half))

    def pass_on(r):
        for c, (lo, count) in enumerate(chunks):
            for half in range(2):
                diagonal(r, c, half).wait_recv()
                spot, out = (at_x, fwd_x) if half == 0 else (at_y, fwd_y)
                for i in range(lo, lo + count):
                    out[r, i] = (
                        part[r, i, spot, half].astype(jnp.float32)
                        + diag_in[r, i, half].astype(jnp.float32)
                    ).astype(jnp.bfloat16)
                start(passed(r, c, half))

    def send_home(r):
        for c, (lo, count) in enumerate(chunks):
            for half in range(2):
                direct(r, c, half).wait_recv()
                passed(r, c, half).wait_recv()
            for i in range(lo, lo + count):
                zsum[r, i] = (
                    part[r, i, xy].astype(jnp.float32) + in_x[r, i].astype(jnp.float32)
                    + in_y[r, i].astype(jnp.float32)
                ).astype(jnp.bfloat16)
            for k in (r + 2, r):
                start(homeward(r, c, k))

    arrived(0, 0, 1)
    arrived(1, 0, 0)
    arrived(0, 2, 1)
    arrived(1, 2, 0)
    for copy in weights:
        copy.wait()
    hidden_a, grad_both = compute(0)
    send_shares(0, grad_both)
    for k in (1, 3):
        for kind in range(2):
            arrived(0, k, kind)
            arrived(1, k, kind)
    for k in (0, 2):
        for kind in range(2):
            corner_over_z(k, kind).wait_recv()
    hidden_b, grad_both = compute(1)
    pass_on(0)
    send_shares(1, grad_both)
    hidden_t = jnp.transpose(jnp.concatenate([hidden_a, hidden_b], axis=0)).astype(jnp.bfloat16)

    def down_piece(q):
        down_v[:, q * piece:(q + 1) * piece] = jnp.dot(
            hidden_t, gf[q], preferred_element_type=jnp.float32
        ).astype(jnp.bfloat16)

    send_home(0)
    for q in range(PIECES // 2):
        down_piece(q)
    pass_on(1)
    for q in range(PIECES // 2, PIECES):
        down_piece(q)
    send_home(1)

    plain_copy.wait_recv()
    pick_copy.wait_recv()
    rows_v[slots:, :width] = jnp.zeros((rows_v.shape[0] - slots, width), jnp.float32)
    for c, (lo, count) in enumerate(chunks):
        for k in range(4):
            homeward(k % 2, c, k).wait_recv()
        for i in range(lo, lo + count):
            total = plain_in[1, i].astype(jnp.float32)
            for k in range(4):
                total = total + in_z[k, i].astype(jnp.float32)
            for q in range(PIECES):
                rows_v[i:i + 1, q * piece:(q + 1) * piece] = total[q:q + 1, :]
    base_copy.wait_recv()
    for copy in sent:
        copy.wait_send()


def group_work(inputs, grads, gate_cols, up_cols, down_rows, route, gate):
    tok, width = inputs.shape
    block = gate_cols.shape[1]
    piece = width // PIECES
    bf16 = jnp.bfloat16
    whole = pl.BlockSpec(memory_space=pl.ANY)
    near = pl.BlockSpec(memory_space=pltpu.VMEM)
    dma = pltpu.SemaphoreType.DMA
    pairs = pltpu.VMEM((2, CAP, 2, PIECES, piece), bf16)
    singles = pltpu.VMEM((2, CAP, PIECES, piece), bf16)
    return pl.pallas_call(
        group_kernel,
        out_shape=(
            pltpu.VMEM((8, width + tok), jnp.float32),
            pltpu.VMEM((tok, width), bf16),
            pltpu.VMEM((block, width), bf16),
        ),
        in_specs=[whole] * 7,
        out_specs=(near, near, near),
        scratch_shapes=[
            pltpu.VMEM(route.shape[::-1], jnp.int32),
            pltpu.VMEM(gate.shape[::-1], jnp.float32),
            pltpu.VMEM((8, tok), jnp.float32),
            pltpu.VMEM((tok, width), bf16),
            pltpu.VMEM((tok, width), bf16),
            pltpu.VMEM((width, 2 * block), bf16),
            pltpu.VMEM((block, width), bf16),
            pltpu.VMEM((CAP, PIECES, piece), jnp.float32),
            pltpu.VMEM((CAP, PIECES, piece), jnp.float32),
            singles,
            pltpu.VMEM((2, SHARDS, CAP, PIECES, piece), bf16),
            pltpu.VMEM((PIECES, CAP * SHARDS, piece), bf16),
            pltpu.VMEM((PIECES, CAP * SHARDS, piece), bf16),
            pltpu.VMEM((2, CAP, 8 * PIECES, piece), bf16),
            pltpu.VMEM((2, CAP, 4, 2, PIECES, piece), bf16),
            pairs,
            singles,
            singles,
            pairs,
            pairs,
            pairs,
            pltpu.VMEM((4, CAP, PIECES, piece), bf16),
            dma((5 + 2 * PIECES,)), dma((4, 2)), dma((4, 2)), dma((2, 4, 2)),
            dma((2, 4, 2)), dma((2, 2)), dma((2, 2)), dma((2, 2)), dma((2, 2)), dma, dma, dma, dma,
            dma, dma,
            dma((2, 2, 4)), dma((2, 2, 4)), dma((2, 2, 2)), dma((2, 2, 2)),
            dma((2, 4)), dma((2, 4)),
        ],
        compiler_params=pltpu.CompilerParams(
            collective_id=0, has_side_effects=True, vmem_limit_bytes=40 * 2**20
        ),
        cost_estimate=pl.CostEstimate(
            flops=12 * CAP * SHARDS * width * block, bytes_accessed=14 * tok * width,
            transcendentals=CAP * SHARDS * block,
        ),
        name="relay_group",
    )(*(
        pltpu.with_memory_space_constraint(operand, pltpu.HBM)
        for operand in (
            inputs, grads, gate_cols, up_cols, down_rows, route.T, gate.T,
        )
    ))


def finish_kernel(rows_v, base_v, down_v, handed_out, down_out, done_v, sem, down_sem):
    width = base_v.shape[1]
    piece = width // PIECES
    halves = down_v.shape[0] // 2
    downs = [
        pltpu.make_async_copy(down_v.at[pl.ds(h * halves, halves)],
                              down_out.at[pl.ds(h * halves, halves)], down_sem.at[h])
        for h in range(2)
    ]
    for copy in downs:
        copy.start()
    stores = [
        pltpu.make_async_copy(done_v.at[:, pl.ds(q * piece, piece)],
                              handed_out.at[:, pl.ds(q * piece, piece)], sem.at[q])
        for q in range(PIECES)
    ]
    named = jnp.transpose(rows_v[:, width:])
    changed = jnp.sum(named, axis=1, keepdims=True) > 0.0
    named = named.astype(jnp.bfloat16)
    for q in range(PIECES):
        at = slice(q * piece, (q + 1) * piece)
        placed = jnp.dot(
            named, rows_v[:, at].astype(jnp.bfloat16), preferred_element_type=jnp.float32
        )
        done_v[:, at] = jnp.where(changed, placed, base_v[:, at].astype(jnp.float32)).astype(
            jnp.bfloat16
        )
        stores[q].start()
    for copy in stores + downs:
        copy.wait()


def finish(rows, base, down):
    whole = pl.BlockSpec(memory_space=pl.ANY)
    near = pl.BlockSpec(memory_space=pltpu.VMEM)
    return pl.pallas_call(
        finish_kernel,
        out_shape=(
            jax.ShapeDtypeStruct(base.shape, base.dtype),
            jax.ShapeDtypeStruct(down.shape, down.dtype),
        ),
        in_specs=[near] * 3,
        out_specs=(whole, whole),
        scratch_shapes=[
            pltpu.VMEM(base.shape, base.dtype),
            pltpu.SemaphoreType.DMA((PIECES,)),
            pltpu.SemaphoreType.DMA((2,)),
        ],
        compiler_params=pltpu.CompilerParams(vmem_limit_bytes=24 * 2**20),
        cost_estimate=pl.CostEstimate(
            flops=16 * base.size, bytes_accessed=4 * base.size, transcendentals=0
        ),
        name="relay_finish",
    )(rows, base, down)


def plain_work(rows, gate_cols, up_cols, down_rows):
    width = lax.axis_size("expert")
    live = width // SHARDS
    across = [[g * SHARDS + j for g in range(live)] for j in range(SHARDS)]
    within = [[g * SHARDS + j for j in range(SHARDS)] for g in range(live)]
    kinds, count, model_width = rows.shape
    if live > 1:
        rows = lax.all_to_all(
            rows, "expert", split_axis=1, concat_axis=1, tiled=True, axis_index_groups=across
        )
    got = lax.all_gather(rows, "expert", axis=1, tiled=True, axis_index_groups=within)
    flat_in, flat_grad = got[0], got[1]
    gate_pre = jnp.dot(flat_in, gate_cols, preferred_element_type=jnp.float32)
    up_pre = jnp.dot(flat_in, up_cols, preferred_element_type=jnp.float32)
    back = lax.dot_general(flat_grad, down_rows, CONTRACT_LAST, preferred_element_type=jnp.float32)
    hidden, grad_gate, grad_up = hidden_grads(gate_pre, up_pre, back)
    share = lax.dot_general(
        grad_gate.astype(jnp.bfloat16), gate_cols, CONTRACT_LAST,
        preferred_element_type=jnp.float32,
    ) + lax.dot_general(
        grad_up.astype(jnp.bfloat16), up_cols, CONTRACT_LAST, preferred_element_type=jnp.float32
    )
    summed = lax.psum_scatter(
        share.astype(jnp.bfloat16), "expert", scatter_dimension=0, tiled=True,
        axis_index_groups=within,
    )
    if live > 1:
        summed = lax.all_to_all(
            summed, "expert", split_axis=0, concat_axis=0, tiled=True, axis_index_groups=across
        )
    down_part = lax.dot_general(
        hidden.astype(jnp.bfloat16), flat_grad, ROWS_FIRST, preferred_element_type=jnp.float32
    ).astype(jnp.bfloat16)
    return summed, down_part


def slot_picks(route, gate, live):
    hit = route[:, :, None] == jnp.arange(live, dtype=jnp.int32)
    member = jnp.sum(hit.astype(jnp.int32), axis=1)
    weight = jnp.sum(jnp.where(hit, gate[:, :, None], 0.0), axis=1)
    position = jnp.cumsum(member, axis=0) - member
    pick = (member[:, :, None] == 1) & (
        position[:, :, None] == jnp.arange(CAP, dtype=jnp.int32)
    )
    return member, weight, pick


def other_core(value):
    return lax.ppermute(value, "pipe", [(0, 1), (1, 0)])


def body(section_inputs, output_grads, w_gate, w_up, w_down, route_ids, route_gates):
    inputs, grads, route, gate = section_inputs[0], output_grads[0], route_ids[0], route_gates[0]
    gate_cols, up_cols, down_rows = w_gate[0], w_up[0], w_down[0]
    tok_rows = inputs.shape[0]
    live = lax.axis_size("expert") // SHARDS
    if live == 1:
        rows, base, down_part = group_work(
            inputs, grads, gate_cols, up_cols, down_rows, route, gate
        )
        handed, down_part = finish(rows, base, down_part)
        return handed[None], down_part[None]
    _, weight, pick = slot_picks(route, gate, live)
    pick_mat = pick.astype(jnp.bfloat16).reshape(tok_rows, live * CAP)
    rows_in = lax.dot_general(pick_mat, inputs, ROWS_FIRST, preferred_element_type=jnp.float32)
    chosen = lax.dot_general(pick_mat, grads, ROWS_FIRST, preferred_element_type=jnp.float32)
    slot_gate = jnp.sum(pick.astype(jnp.float32) * weight[:, :, None], axis=0).reshape(-1, 1)
    rows = jnp.stack([rows_in.astype(jnp.bfloat16), (chosen * slot_gate).astype(jnp.bfloat16)])
    summed, down_part = plain_work(rows, gate_cols, up_cols, down_rows)
    branch = jnp.dot(pick_mat, summed, preferred_element_type=jnp.float32)
    input_grad = (grads.astype(jnp.float32) + branch).astype(jnp.bfloat16)
    return other_core(input_grad)[None], down_part[None]


def solution(mesh):
    return jax.shard_map(
        body,
        mesh=mesh,
        in_specs=(
            P("pipe", "expert", None),
            P("pipe", "expert", None),
            P("pipe", None, "expert"),
            P("pipe", None, "expert"),
            P("pipe", "expert", None),
            P("pipe", "expert", None),
            P("pipe", "expert", None),
        ),
        out_specs=(P("pipe", "expert", None), P("pipe", "expert", None)),
        check_vma=False,
    )
```

```python
import jax
import jax.numpy as jnp
from jax import lax
from jax.experimental import pallas as pl
from jax.experimental.pallas import tpu as pltpu
from jax.sharding import PartitionSpec as P

SHARDS = 16
CAP = 5
PIECES = 8
MESH = pl.DeviceIdType.MESH
CONTRACT_LAST = (((1,), (1,)), ((), ()))
ROWS_FIRST = (((0,), (0,)), ((), ()))


def hidden_grads(gate_pre, up_pre, back_hidden):
    sigma = jax.nn.sigmoid(gate_pre)
    silu_gate = gate_pre * sigma
    hidden = silu_gate * up_pre
    grad_gate = back_hidden * up_pre * sigma * (1.0 + gate_pre * (1.0 - sigma))
    grad_up = back_hidden * silu_gate
    return hidden, grad_gate, grad_up


def flip(z, k):
    if k == 0:
        return z
    if k == 1:
        return z + 1 - 2 * lax.rem(z, 2)
    if k == 2:
        return lax.rem(z + 2, 4)
    return 3 - z


def pick_slots(route, gate):
    tok = route.shape[1]
    hit = route == 0
    member = jnp.sum(jnp.where(hit, 1.0, 0.0), axis=0, keepdims=True)
    earlier = lax.broadcasted_iota(jnp.int32, (tok, tok), 0) < lax.broadcasted_iota(
        jnp.int32, (tok, tok), 1
    )
    member8 = jnp.broadcast_to(member, (8, tok))
    position = jnp.dot(
        member8.astype(jnp.bfloat16),
        jnp.where(earlier, 1.0, 0.0).astype(jnp.bfloat16),
        preferred_element_type=jnp.float32,
    )
    slot = lax.broadcasted_iota(jnp.int32, (8, tok), 0).astype(jnp.float32)
    pick = jnp.where((member8 == 1.0) & (position == slot), 1.0, 0.0)
    weight = jnp.sum(jnp.where(hit, gate, 0.0), axis=0, keepdims=True)
    return pick, jnp.sum(pick * weight, axis=1, keepdims=True)


def swap_order(outer, inner):
    size = outer * inner
    r = lax.broadcasted_iota(jnp.int32, (size, size), 0)
    c = lax.broadcasted_iota(jnp.int32, (size, size), 1)
    source = lax.rem(r, outer) * inner + r // outer
    return jnp.where(c == source, 1.0, 0.0).astype(jnp.bfloat16)


def group_kernel(
    x_hbm, g_hbm, wg_hbm, wu_hbm, wd_hbm, route_hbm, gate_hbm,
    rows_v, base_v, down_v,
    route_v, gate_v, pick_v, x_v, g_v, wgu, wd_v, staged, plain, plain_in, gath, xf, gf, pfull, part,
    diag_in, fwd_x, fwd_y, in_x, in_y, zsum, in_z,
    load_sem, z_send, z_recv, xy_send, xy_recv, d_send, d_recv, dz_send, dz_recv,
    p_send, p_recv, t_send, t_recv, b_send, b_recv, s1_send, s1_recv, s2_send, s2_recv, s3_send, s3_recv,
):
    slots, piece = staged.shape[0], staged.shape[2]
    block = wd_v.shape[0]
    pipe = lax.axis_index("pipe")
    me = lax.axis_index("expert")
    base = (me // SHARDS) * SHARDS
    local = lax.rem(me, SHARDS)
    z = local // 4
    xy = lax.rem(local, 4)
    y, x = xy // 2, lax.rem(xy, 2)
    at_x, at_y, at_d = y * 2 + 1 - x, (1 - y) * 2 + x, 3 - xy

    def device(p, zz, spot):
        return {"pipe": p, "expert": base + zz * 4 + spot}

    x_dev, y_dev = device(pipe, z, at_x), device(pipe, z, at_y)
    z_dev = [device(pipe, flip(z, k), xy) for k in range(4)]
    back_dev = [device(1 - pipe, flip(z, k), xy) for k in range(4)]

    barrier = pltpu.get_barrier_semaphore()
    for other in [x_dev, y_dev] + z_dev[1:] + back_dev:
        pl.semaphore_signal(barrier, inc=1, device_id=other, device_id_type=MESH)

    def cols(q):
        return pl.ds(q * piece, piece)

    small = [
        pltpu.make_async_copy(route_hbm, route_v, load_sem.at[0]),
        pltpu.make_async_copy(gate_hbm, gate_v, load_sem.at[1]),
    ]
    row_loads = [
        [
            pltpu.make_async_copy(src.at[:, cols(q)], dst.at[:, cols(q)],
                                  load_sem.at[5 + kind * PIECES + q])
            for q in range(PIECES)
        ]
        for kind, (src, dst) in enumerate(((x_hbm, x_v), (g_hbm, g_v)))
    ]
    weights = [
        pltpu.make_async_copy(wg_hbm, wgu.at[:, :, pl.ds(0, block)], load_sem.at[2]),
        pltpu.make_async_copy(wu_hbm, wgu.at[:, :, pl.ds(block, block)], load_sem.at[3]),
        pltpu.make_async_copy(wd_hbm, wd_v, load_sem.at[4]),
    ]
    for copy in small + row_loads[0] + row_loads[1]:
        copy.start()
    for copy in small:
        copy.wait()
    pick, coef = pick_slots(route_v[...], gate_v[...])
    pick_v[...] = pick
    pick_mat = pick.astype(jnp.bfloat16)

    for kind in range(2):
        source = x_v if kind == 0 else g_v
        for q in range(PIECES):
            row_loads[kind][q].wait()
            rows = jnp.dot(
                pick_mat, source[:, q * piece:(q + 1) * piece], preferred_element_type=jnp.float32
            )
            scaled = rows if kind == 0 else rows * coef
            for i in range(slots):
                staged[i, kind * PIECES + q:kind * PIECES + q + 1, :] = scaled[i:i + 1, :]
                if kind == 1:
                    plain[i, q:q + 1, :] = rows[i:i + 1, :]

    def index(spot, k):
        return (k % 2) * 8 + spot * 2 + lax.rem(z // 2 + k // 2, 2)

    own = index(xy, 0)
    for i in range(slots):
        gath[own, i] = staged[i].astype(jnp.bfloat16)
    plain_in[0] = plain[...].astype(jnp.bfloat16)
    for copy in weights:
        copy.start()
    pl.semaphore_wait(barrier, 9)

    def remote(src, dst, send, recv, to):
        return pltpu.make_async_remote_copy(
            src_ref=src, dst_ref=dst, send_sem=send, recv_sem=recv, device_id=to,
            device_id_type=MESH,
        )

    sent = []

    def start(copy):
        copy.start()
        sent.append(copy)
        return copy

    for k in (2, 1, 3):
        start(remote(gath.at[own], gath.at[(k % 2) * 8 + xy * 2 + z // 2],
                     z_send.at[k], z_recv.at[k], z_dev[k]))

    def halves(k):
        if k % 2 == 1:
            return (pl.ds(0, slots),)
        cut = 3 if k == 0 else 2
        return (pl.ds(0, cut), pl.ds(cut, slots - cut))

    def slab(spot, k, half):
        return gath.at[index(spot, k), halves(k)[half]]

    def over(axis, k, half):
        ref = slab(xy, k, half)
        return remote(ref, ref, xy_send.at[axis, k, half], xy_recv.at[axis, k, half],
                      x_dev if axis == 0 else y_dev)

    def to_plane(k):
        if k % 2 == 1:
            start(over(0, k, 0))
            start(over(1, k, 0))
        else:
            start(over(0, k, 0))
            start(over(1, k, 1))
            start(over(0, k, 1))
            start(over(1, k, 0))

    def arrived(axis, k, half):
        ref = slab(at_x if axis == 0 else at_y, k, half)
        remote(ref, ref, xy_send.at[axis, k, half], xy_recv.at[axis, k, half], x_dev).wait_recv()

    def to_corner(k):
        arrived(0, k, 0)
        ref = slab(at_x, k, 0)
        start(remote(ref, ref, d_send.at[k // 2, 0], d_recv.at[k // 2, 0], y_dev))
        arrived(1, k, 1)
        ref = slab(at_y, k, 1)
        start(remote(ref, ref, d_send.at[k // 2, 1], d_recv.at[k // 2, 1], x_dev))

    def corner_arrived(k):
        for half in range(2):
            ref = slab(at_d, k, half)
            remote(ref, ref, d_send.at[k // 2, half], d_recv.at[k // 2, half], y_dev).wait_recv()

    def z_arrived(k):
        ref = gath.at[index(xy, k)]
        remote(ref, ref, z_send.at[k], z_recv.at[k], z_dev[k]).wait_recv()

    def corner_over_z(k):
        source = index(at_d, k)
        return remote(gath.at[source], gath.at[8 + source], dz_send.at[k // 2],
                      dz_recv.at[k // 2], z_dev[1])

    to_plane(0)
    plain_copy = start(remote(plain_in.at[0], plain_in.at[1], p_send, p_recv, back_dev[0]))
    width = x_v.shape[1]
    pick_copy = start(
        remote(pick_v, rows_v.at[:, pl.ds(width, pick_v.shape[1])], t_send, t_recv, back_dev[0])
    )
    z_arrived(2)
    to_plane(2)
    to_corner(0)
    to_corner(2)
    z_arrived(1)
    to_plane(1)
    corner_arrived(0)
    start(corner_over_z(0))
    z_arrived(3)
    to_plane(3)
    corner_arrived(2)
    start(corner_over_z(2))

    group_rows = slots * 8
    to_rows = swap_order(8, 2 * PIECES)
    to_units = swap_order(PIECES, 8)
    chunks = ((0, 3), (3, slots - 3))

    def compute(r):
        for i in range(slots):
            packed = gath[r * 8:(r + 1) * 8, i].reshape(8 * 2 * PIECES, piece)
            ordered = jnp.dot(to_rows, packed, preferred_element_type=jnp.float32)
            at = r * group_rows + i * 8
            for q in range(PIECES):
                xf[q, at:at + 8, :] = ordered[q * 8:(q + 1) * 8].astype(jnp.bfloat16)
                gf[q, at:at + 8, :] = ordered[
                    (PIECES + q) * 8:(PIECES + q + 1) * 8
                ].astype(jnp.bfloat16)
        mine = slice(r * group_rows, (r + 1) * group_rows)
        pre = jnp.zeros((group_rows, 2 * block), jnp.float32)
        back = jnp.zeros((group_rows, block), jnp.float32)
        for q in range(PIECES):
            pre = pre + jnp.dot(xf[q, mine, :], wgu[q], preferred_element_type=jnp.float32)
            back = back + lax.dot_general(
                gf[q, mine, :], wd_v[:, q * piece:(q + 1) * piece], CONTRACT_LAST,
                preferred_element_type=jnp.float32,
            )
        hidden, grad_gate, grad_up = hidden_grads(pre[:, :block], pre[:, block:], back)
        grad_both = jnp.concatenate(
            [grad_gate.astype(jnp.bfloat16), grad_up.astype(jnp.bfloat16)], axis=1
        )
        return hidden, grad_both

    def diagonal(r, c, half):
        lo, count = chunks[c]
        at = pl.ds(lo, count)
        return remote(part.at[r, at, at_d, half], diag_in.at[r, at, half],
                      s1_send.at[r, c, half], s1_recv.at[r, c, half],
                      y_dev if half == 0 else x_dev)

    def direct(r, c, half):
        lo, count = chunks[c]
        at = pl.ds(lo, count)
        if half == 1:
            return remote(part.at[r, at, at_x, 1], in_x.at[r, at, 1], s1_send.at[r, c, 2],
                          s1_recv.at[r, c, 2], x_dev)
        return remote(part.at[r, at, at_y, 0], in_y.at[r, at, 0], s1_send.at[r, c, 3],
                      s1_recv.at[r, c, 3], y_dev)

    def passed(r, c, half):
        lo, count = chunks[c]
        at = pl.ds(lo, count)
        if half == 0:
            return remote(fwd_x.at[r, at], in_x.at[r, at, 0], s2_send.at[r, c, 0],
                          s2_recv.at[r, c, 0], x_dev)
        return remote(fwd_y.at[r, at], in_y.at[r, at, 1], s2_send.at[r, c, 1],
                      s2_recv.at[r, c, 1], y_dev)

    def homeward(r, c, k):
        lo, count = chunks[c]
        at = pl.ds(lo, count)
        return remote(zsum.at[r, at, lax.rem(z // 2 + k // 2, 2)], in_z.at[k, at],
                      s3_send.at[c, k], s3_recv.at[c, k], back_dev[k])

    def send_shares(r, grad_both):
        for q in range(PIECES):
            share = lax.dot_general(
                grad_both, wgu[q], CONTRACT_LAST, preferred_element_type=jnp.float32
            ).astype(jnp.bfloat16)
            for i in range(slots):
                pfull[r, i, q * 8:(q + 1) * 8, :] = share[i * 8:(i + 1) * 8]
        for c, (lo, count) in enumerate(chunks):
            for i in range(lo, lo + count):
                units = jnp.dot(to_units, pfull[r, i], preferred_element_type=jnp.float32)
                part[r, i] = units.reshape(4, 2, PIECES, piece).astype(jnp.bfloat16)
            for half in range(2):
                start(diagonal(r, c, half))
        for c in range(2):
            for half in range(2):
                start(direct(r, c, half))

    def pass_on(r):
        for c, (lo, count) in enumerate(chunks):
            for half in range(2):
                diagonal(r, c, half).wait_recv()
                spot, out = (at_x, fwd_x) if half == 0 else (at_y, fwd_y)
                for i in range(lo, lo + count):
                    out[r, i] = (
                        part[r, i, spot, half].astype(jnp.float32)
                        + diag_in[r, i, half].astype(jnp.float32)
                    ).astype(jnp.bfloat16)
                start(passed(r, c, half))

    def send_home(r):
        for c, (lo, count) in enumerate(chunks):
            for half in range(2):
                direct(r, c, half).wait_recv()
                passed(r, c, half).wait_recv()
            for i in range(lo, lo + count):
                zsum[r, i] = (
                    part[r, i, xy].astype(jnp.float32) + in_x[r, i].astype(jnp.float32)
                    + in_y[r, i].astype(jnp.float32)
                ).astype(jnp.bfloat16)
            for k in (r + 2, r):
                start(homeward(r, c, k))

    arrived(0, 0, 1)
    arrived(1, 0, 0)
    arrived(0, 2, 1)
    arrived(1, 2, 0)
    for copy in weights:
        copy.wait()
    hidden_a, grad_both = compute(0)
    send_shares(0, grad_both)
    for k in (1, 3):
        arrived(0, k, 0)
        arrived(1, k, 0)
    for k in (0, 2):
        corner_over_z(k).wait_recv()
    base_copy = start(remote(g_v, base_v, b_send, b_recv, back_dev[0]))
    hidden_b, grad_both = compute(1)
    pass_on(0)
    send_shares(1, grad_both)
    hidden_t = jnp.transpose(jnp.concatenate([hidden_a, hidden_b], axis=0)).astype(jnp.bfloat16)

    def down_piece(q):
        down_v[:, q * piece:(q + 1) * piece] = jnp.dot(
            hidden_t, gf[q], preferred_element_type=jnp.float32
        ).astype(jnp.bfloat16)

    send_home(0)
    for q in range(2):
        down_piece(q)
    pass_on(1)
    for q in range(2, 5):
        down_piece(q)
    send_home(1)
    for q in range(5, PIECES):
        down_piece(q)

    plain_copy.wait_recv()
    pick_copy.wait_recv()
    rows_v[slots:, :width] = jnp.zeros((rows_v.shape[0] - slots, width), jnp.float32)
    for c, (lo, count) in enumerate(chunks):
        for k in range(4):
            homeward(k % 2, c, k).wait_recv()
        for i in range(lo, lo + count):
            total = plain_in[1, i].astype(jnp.float32)
            for k in range(4):
                total = total + in_z[k, i].astype(jnp.float32)
            for q in range(PIECES):
                rows_v[i:i + 1, q * piece:(q + 1) * piece] = total[q:q + 1, :]
    base_copy.wait_recv()
    for copy in sent:
        copy.wait_send()


def group_work(inputs, grads, gate_cols, up_cols, down_rows, route, gate):
    tok, width = inputs.shape
    block = gate_cols.shape[1]
    piece = width // PIECES
    bf16 = jnp.bfloat16
    whole = pl.BlockSpec(memory_space=pl.ANY)
    near = pl.BlockSpec(memory_space=pltpu.VMEM)
    dma = pltpu.SemaphoreType.DMA
    pairs = pltpu.VMEM((2, CAP, 2, PIECES, piece), bf16)
    singles = pltpu.VMEM((2, CAP, PIECES, piece), bf16)
    return pl.pallas_call(
        group_kernel,
        out_shape=(
            pltpu.VMEM((8, width + tok), jnp.float32),
            pltpu.VMEM((tok, width), bf16),
            pltpu.VMEM((block, width), bf16),
        ),
        in_specs=[whole] * 7,
        out_specs=(near, near, near),
        scratch_shapes=[
            pltpu.VMEM(route.shape[::-1], jnp.int32),
            pltpu.VMEM(gate.shape[::-1], jnp.float32),
            pltpu.VMEM((8, tok), jnp.float32),
            pltpu.VMEM((tok, width), bf16),
            pltpu.VMEM((tok, width), bf16),
            pltpu.VMEM((PIECES, piece, 2 * block), bf16),
            pltpu.VMEM((block, width), bf16),
            pltpu.VMEM((CAP, 2 * PIECES, piece), jnp.float32),
            pltpu.VMEM((CAP, PIECES, piece), jnp.float32),
            singles,
            pltpu.VMEM((SHARDS, CAP, 2 * PIECES, piece), bf16),
            pltpu.VMEM((PIECES, CAP * SHARDS, piece), bf16),
            pltpu.VMEM((PIECES, CAP * SHARDS, piece), bf16),
            pltpu.VMEM((2, CAP, 8 * PIECES, piece), bf16),
            pltpu.VMEM((2, CAP, 4, 2, PIECES, piece), bf16),
            pairs,
            singles,
            singles,
            pairs,
            pairs,
            pairs,
            pltpu.VMEM((4, CAP, PIECES, piece), bf16),
            dma((5 + 2 * PIECES,)), dma((4,)), dma((4,)), dma((2, 4, 2)),
            dma((2, 4, 2)), dma((2, 2)), dma((2, 2)), dma((2,)), dma((2,)), dma, dma, dma, dma,
            dma, dma,
            dma((2, 2, 4)), dma((2, 2, 4)), dma((2, 2, 2)), dma((2, 2, 2)),
            dma((2, 4)), dma((2, 4)),
        ],
        compiler_params=pltpu.CompilerParams(
            collective_id=0, has_side_effects=True, vmem_limit_bytes=40 * 2**20
        ),
        cost_estimate=pl.CostEstimate(
            flops=12 * CAP * SHARDS * width * block, bytes_accessed=14 * tok * width,
            transcendentals=CAP * SHARDS * block,
        ),
        name="relay_group",
    )(*(
        pltpu.with_memory_space_constraint(operand, pltpu.HBM)
        for operand in (
            inputs, grads, gate_cols.reshape(PIECES, piece, block),
            up_cols.reshape(PIECES, piece, block), down_rows, route.T, gate.T,
        )
    ))


def finish_kernel(rows_v, base_v, down_v, handed_out, down_out, done_v, sem, down_sem):
    width = base_v.shape[1]
    piece = width // PIECES
    halves = down_v.shape[0] // 2
    downs = [
        pltpu.make_async_copy(down_v.at[pl.ds(h * halves, halves)],
                              down_out.at[pl.ds(h * halves, halves)], down_sem.at[h])
        for h in range(2)
    ]
    for copy in downs:
        copy.start()
    stores = [
        pltpu.make_async_copy(done_v.at[:, pl.ds(q * piece, piece)],
                              handed_out.at[:, pl.ds(q * piece, piece)], sem.at[q])
        for q in range(PIECES)
    ]
    named = jnp.transpose(rows_v[:, width:])
    changed = jnp.sum(named, axis=1, keepdims=True) > 0.0
    named = named.astype(jnp.bfloat16)
    for q in range(PIECES):
        at = slice(q * piece, (q + 1) * piece)
        placed = jnp.dot(
            named, rows_v[:, at].astype(jnp.bfloat16), preferred_element_type=jnp.float32
        )
        done_v[:, at] = jnp.where(changed, placed, base_v[:, at].astype(jnp.float32)).astype(
            jnp.bfloat16
        )
        stores[q].start()
    for copy in stores + downs:
        copy.wait()


def finish(rows, base, down):
    whole = pl.BlockSpec(memory_space=pl.ANY)
    near = pl.BlockSpec(memory_space=pltpu.VMEM)
    return pl.pallas_call(
        finish_kernel,
        out_shape=(
            jax.ShapeDtypeStruct(base.shape, base.dtype),
            jax.ShapeDtypeStruct(down.shape, down.dtype),
        ),
        in_specs=[near] * 3,
        out_specs=(whole, whole),
        scratch_shapes=[
            pltpu.VMEM(base.shape, base.dtype),
            pltpu.SemaphoreType.DMA((PIECES,)),
            pltpu.SemaphoreType.DMA((2,)),
        ],
        compiler_params=pltpu.CompilerParams(vmem_limit_bytes=24 * 2**20),
        cost_estimate=pl.CostEstimate(
            flops=16 * base.size, bytes_accessed=4 * base.size, transcendentals=0
        ),
        name="relay_finish",
    )(rows, base, down)


def plain_work(rows, gate_cols, up_cols, down_rows):
    width = lax.axis_size("expert")
    live = width // SHARDS
    across = [[g * SHARDS + j for g in range(live)] for j in range(SHARDS)]
    within = [[g * SHARDS + j for j in range(SHARDS)] for g in range(live)]
    kinds, count, model_width = rows.shape
    if live > 1:
        rows = lax.all_to_all(
            rows, "expert", split_axis=1, concat_axis=1, tiled=True, axis_index_groups=across
        )
    got = lax.all_gather(rows, "expert", axis=1, tiled=True, axis_index_groups=within)
    flat_in, flat_grad = got[0], got[1]
    gate_pre = jnp.dot(flat_in, gate_cols, preferred_element_type=jnp.float32)
    up_pre = jnp.dot(flat_in, up_cols, preferred_element_type=jnp.float32)
    back = lax.dot_general(flat_grad, down_rows, CONTRACT_LAST, preferred_element_type=jnp.float32)
    hidden, grad_gate, grad_up = hidden_grads(gate_pre, up_pre, back)
    share = lax.dot_general(
        grad_gate.astype(jnp.bfloat16), gate_cols, CONTRACT_LAST,
        preferred_element_type=jnp.float32,
    ) + lax.dot_general(
        grad_up.astype(jnp.bfloat16), up_cols, CONTRACT_LAST, preferred_element_type=jnp.float32
    )
    summed = lax.psum_scatter(
        share.astype(jnp.bfloat16), "expert", scatter_dimension=0, tiled=True,
        axis_index_groups=within,
    )
    if live > 1:
        summed = lax.all_to_all(
            summed, "expert", split_axis=0, concat_axis=0, tiled=True, axis_index_groups=across
        )
    down_part = lax.dot_general(
        hidden.astype(jnp.bfloat16), flat_grad, ROWS_FIRST, preferred_element_type=jnp.float32
    ).astype(jnp.bfloat16)
    return summed, down_part


def slot_picks(route, gate, live):
    hit = route[:, :, None] == jnp.arange(live, dtype=jnp.int32)
    member = jnp.sum(hit.astype(jnp.int32), axis=1)
    weight = jnp.sum(jnp.where(hit, gate[:, :, None], 0.0), axis=1)
    position = jnp.cumsum(member, axis=0) - member
    pick = (member[:, :, None] == 1) & (
        position[:, :, None] == jnp.arange(CAP, dtype=jnp.int32)
    )
    return member, weight, pick


def other_core(value):
    return lax.ppermute(value, "pipe", [(0, 1), (1, 0)])


def body(section_inputs, output_grads, w_gate, w_up, w_down, route_ids, route_gates):
    inputs, grads, route, gate = section_inputs[0], output_grads[0], route_ids[0], route_gates[0]
    gate_cols, up_cols, down_rows = w_gate[0], w_up[0], w_down[0]
    tok_rows = inputs.shape[0]
    live = lax.axis_size("expert") // SHARDS
    if live == 1:
        rows, base, down_part = group_work(
            inputs, grads, gate_cols, up_cols, down_rows, route, gate
        )
        handed, down_part = finish(rows, base, down_part)
        return handed[None], down_part[None]
    _, weight, pick = slot_picks(route, gate, live)
    pick_mat = pick.astype(jnp.bfloat16).reshape(tok_rows, live * CAP)
    rows_in = lax.dot_general(pick_mat, inputs, ROWS_FIRST, preferred_element_type=jnp.float32)
    chosen = lax.dot_general(pick_mat, grads, ROWS_FIRST, preferred_element_type=jnp.float32)
    slot_gate = jnp.sum(pick.astype(jnp.float32) * weight[:, :, None], axis=0).reshape(-1, 1)
    rows = jnp.stack([rows_in.astype(jnp.bfloat16), (chosen * slot_gate).astype(jnp.bfloat16)])
    summed, down_part = plain_work(rows, gate_cols, up_cols, down_rows)
    branch = jnp.dot(pick_mat, summed, preferred_element_type=jnp.float32)
    input_grad = (grads.astype(jnp.float32) + branch).astype(jnp.bfloat16)
    return other_core(input_grad)[None], down_part[None]


def solution(mesh):
    return jax.shard_map(
        body,
        mesh=mesh,
        in_specs=(
            P("pipe", "expert", None),
            P("pipe", "expert", None),
            P("pipe", None, "expert"),
            P("pipe", None, "expert"),
            P("pipe", "expert", None),
            P("pipe", "expert", None),
            P("pipe", "expert", None),
        ),
        out_specs=(P("pipe", "expert", None), P("pipe", "expert", None)),
        check_vma=False,
    )
```
